256 devices in a mesh: facet: 16 (over z, y_hi), band: 16 (over y_lo, x, core).
Axes of the slice: x: 4, y: 4 (y_hi: 2, y_lo: 2; y = y_hi * 2 + y_lo), z: 8, core: 2. Of those that a mesh axis runs over, the one named last changes fastest.
Arguments:
- visibilities: bfloat16 [16, 256, 2, 1024], P('band', 'facet'), may hold values from -6 to 6
- uv_coords: bfloat16 [16, 256, 2, 64], P('band', 'facet'), may hold values from -0.5 to 0.5
- freq_ratio: float32 [16, 16], P('band'), may hold values from 0.9 to 1.1
- target_facet: int32 [16, 256, 1], P('band', 'facet'), may hold values from 0 to 15; in each aligned block of 16 rows (0 to 15, 16 to 31, ..., all dimensions but the last counted through in order) at most 2 rows name the same one
- tile_index: int32 [16, 256], P('band', 'facet'), may hold values from 0 to 63
Outputs:
- facet_images: float32 [16, 2, 512, 2048], P('facet', None, 'band')
The draws below stay inside these ranges and needn't reach their ends.
Inputs may be any that keep to these rules, and one draw needn't show every extreme that they name: `target_facet`: among the 16 blocks of one subband held by one index of facet (aligned blocks of rows), at most 2 name the same facet.
All inputs are finite; a program needn't handle non-finite values.
Results may differ from the reference program's by a relative error of at most 0.0037.
Values may be sent and summed in bfloat16 or wider, within the bound.
No kernel may reach another device: no remote copies, remote signals or barrier semaphores. Data moves between devices by JAX's collectives and lax.ppermute only.
A program may use at most 64 MiB of HBM per device.

```python
import math
import jax
import jax.numpy as jnp
import numpy as np
from jax import lax

TILE = 128
FCOLS = 2048
FROWS = 512
CH = 16
NV = 64
BLK_DEV = 16
CAP = 2
FACETS = 16
BANDS = 16
BLOCKS = 256
TILES = 64


def set_ends(drawn, rng, least, top_value):
    shape = drawn.shape
    place = [jax.random.randint(jax.random.fold_in(rng, axis), (), 0, shape[axis]) for axis in range(len(shape))]
    drawn = drawn.at[tuple(place)].set(least)
    longest = shape.index(max(shape))
    place[longest] = (place[longest] + 1) % shape[longest]
    return drawn.at[tuple(place)].set(top_value)


def shard_levels(key, dims, cuts, least, high):
    factor_of = 1.0
    for axis_at, shards_of in cuts:
        steps = jax.random.uniform(jax.random.fold_in(jax.random.fold_in(key, 6), axis_at), (shards_of,), jnp.float32, least / len(cuts), high / len(cuts))
        factor_of = factor_of * jnp.repeat(jnp.exp(steps), dims[axis_at] // shards_of).reshape((-1,) + (1,) * (len(dims) - 1 - axis_at))
    return factor_of


def shared_out(rng, own, number, rows, number_of, top, bound, lean):
    order = jax.random.permutation(rng, number_of)
    crowded, usual = shares(number_of, rows * top, bound, lean, True), shares(number_of, rows * top, bound, lean, False)
    places = jnp.arange(number_of)

    def named(tallies, offset_by):
        used = int((tallies > 0).sum())
        fixed = max(1, used // 4)
        passed = fixed + (places - fixed + offset_by * (used - fixed)) % max(1, number_of - fixed)
        return jnp.zeros((number_of,), jnp.int32).at[order[jnp.where(places < fixed, places, passed)]].set(jnp.asarray(tallies, jnp.int32))

    tallies = jnp.where(number % 4 == 0, named(crowded, number // 4), named(usual, number - number // 4 - 1))
    mixed = jax.random.permutation(jax.random.fold_in(own, 3), number_of)
    giver, sink = mixed[0:number_of // 2 * 2:2], mixed[1:number_of // 2 * 2:2]
    slack = jnp.minimum(tallies[giver] - 1, bound - tallies[sink]) // 2
    slack = jnp.where((giver == order[0]) | (sink == order[0]) | (tallies[sink] == 0), 0, jnp.maximum(slack, 0))
    passed = jax.random.randint(jax.random.fold_in(own, 4), (number_of // 2,), 0, 1 << 20) % (slack + 1)
    tallies = tallies.at[giver].add(-passed).at[sink].add(passed)
    members = jnp.searchsorted(jnp.cumsum(tallies), jnp.arange(rows * top), side="right").astype(jnp.int32)
    grid = members.reshape(top, rows).T
    grid = grid[jax.random.permutation(jax.random.fold_in(own, 1), rows)]
    offset_by = jax.random.randint(jax.random.fold_in(own, 2), (rows, 1), 0, top)
    return jnp.take_along_axis(grid, (jnp.arange(top)[None, :] + offset_by) % top, axis=1)


def shares(amount, total, most, skew, full):
    weights = [(1 << 20) // math.isqrt(grade ** skew) + 1 for grade in range(1, amount + 1)]
    largest = most if full else min(most, max(-(-total // amount), total * weights[0] // sum(weights)))
    least = 1 if total - largest >= amount - 1 else 0
    given, surplus = [largest] + [least] * (amount - 1), total - largest - least * (amount - 1)
    while surplus > 0:
        free = [i for i in range(1, amount) if given[i] < largest] or [i for i in range(1, amount) if given[i] < most]
        whole, budget = sum([weights[i] for i in free]), surplus
        for i in free:
            extra = min(most - given[i], max(1, budget * weights[i] // whole), surplus)
            given[i] = given[i] + extra
            surplus = surplus - extra
    return np.array(given)


def centred(own_key, shape, scale, bound, split=(), kind=jnp.bfloat16):
    entries = jax.random.normal(own_key, shape, jnp.float32) * scale
    if len(split) > 0:
        entries = shard_levels(own_key, shape, split, -0.22, 0.18) * entries
    return jnp.clip(entries, min=-bound, max=bound).astype(kind)


def setup_inputs(seed: int = 0) -> dict:
    seeds = jax.random.split(jax.random.key(seed), 6)
    visibilities = centred(seeds[0], (BANDS, BLOCKS, 2, CH * NV), 1.0, 6.0, ((0, 16), (1, 16)))
    uv_coords = jnp.clip(jax.random.uniform(seeds[1], (BANDS, BLOCKS, 2, NV), jnp.float32, -0.5, 0.5) * shard_levels(seeds[1], (BANDS, BLOCKS, 2, NV), ((0, 16), (1, 16)), -0.4, 0.0), -0.5, 0.5).astype(jnp.bfloat16)
    freq_ratio = jnp.clip(0.9 + 0.20000005 * jax.random.uniform(seeds[2], (BANDS, CH), jnp.float32) ** shard_levels(seeds[2], (BANDS, CH), ((0, 16),), -0.2, 0.2), 0.9, 1.1)
    target_facet_keys = jax.random.split(jax.random.fold_in(seeds[3], 1), BANDS * BLOCKS // BLK_DEV)
    target_facet_turns = jax.random.permutation(jax.random.fold_in(seeds[3], 3), BANDS * BLOCKS // BLK_DEV)
    target_facet = jax.vmap(lambda own, number: shared_out(jax.random.fold_in(seeds[3], 2), own, number, BLK_DEV, FACETS, 1, CAP, 2))(target_facet_keys, target_facet_turns).reshape((BANDS, BLOCKS, 1))
    tile_index = set_ends(jax.random.randint(seeds[4], (BANDS, BLOCKS), 0, TILES), jax.random.fold_in(seeds[4], 1), 0, TILES - 1).astype(jnp.int32)
    return {"visibilities": visibilities, "uv_coords": uv_coords, "freq_ratio": freq_ratio, "target_facet": target_facet, "tile_index": tile_index}


TWO_PI = 2.0 * math.pi

def make_tile(block_vis, block_uv, facet_id, tile_id, frequencies):
    channels = frequencies.shape[0]
    samples = block_uv.shape[1]
    tile_span = TILE
    across = FCOLS // tile_span
    tile_row = tile_id // across
    tile_col = tile_id % across
    offsets = jnp.arange(tile_span, dtype=jnp.int32)
    pixel_rows = (FROWS * (facet_id % 4 - 2) + tile_row * tile_span + offsets).astype(jnp.float32)
    pixel_cols = (FCOLS * (facet_id // 4 % 4 - 2) + tile_col * tile_span + offsets).astype(jnp.float32)
    u_scaled = frequencies[:, None] * block_uv[0].astype(jnp.float32)[None, :]
    v_scaled = frequencies[:, None] * block_uv[1].astype(jnp.float32)[None, :]
    phase_l = u_scaled[:, :, None] * pixel_rows * TWO_PI
    phase_m = v_scaled[:, :, None] * pixel_cols * TWO_PI
    real_vis = block_vis[0].astype(jnp.float32).reshape(channels, samples)[:, :, None]
    imag_vis = block_vis[1].astype(jnp.float32).reshape(channels, samples)[:, :, None]
    cos_rows = jnp.cos(phase_l)
    sin_rows = jnp.sin(phase_l)
    real_term = real_vis * cos_rows - imag_vis * sin_rows
    imag_term = real_vis * sin_rows + imag_vis * cos_rows
    taylor_weights = jnp.stack([jnp.ones_like(frequencies), (frequencies - 1.0) * 10.0], axis=1) * (1.0 / math.sqrt(channels * samples))
    weights = taylor_weights[:, None, :, None]
    left_factor = jnp.stack([real_term[:, :, None, :] * weights, -(imag_term[:, :, None, :] * weights)])
    left_factor = left_factor.astype(jnp.bfloat16).reshape(2 * channels * samples, 2 * tile_span)
    right_factor = jnp.stack([jnp.cos(phase_m), jnp.sin(phase_m)]).astype(jnp.bfloat16).reshape(2 * channels * samples, tile_span)
    return lax.dot_general(left_factor, right_factor, (((0,), (0,)), ((), ())), preferred_element_type=jnp.float32)

def reference(visibilities, uv_coords, freq_ratio, target_facet, tile_index):
    across = FCOLS // TILE
    tile_rows = FROWS // TILE
    vis_flat = visibilities.reshape(BANDS * BLOCKS, 2, CH * NV)
    uv_flat = uv_coords.reshape(BANDS * BLOCKS, 2, NV)
    band_of = jnp.repeat(jnp.arange(BANDS, dtype=jnp.int32), BLOCKS)
    facet_flat = target_facet.reshape(BANDS * BLOCKS).astype(jnp.int32)
    tile_flat = tile_index.reshape(BANDS * BLOCKS).astype(jnp.int32)
    facet_image = jnp.zeros((FACETS, 2, tile_rows, across, TILE, TILE), jnp.float32)

    def add_block(totals, block_items):
        block_vis, block_uv, band_id, facet_id, tile_id = block_items
        result = make_tile(block_vis, block_uv, facet_id, tile_id, freq_ratio[band_id]).reshape(2, TILE, TILE)
        totals = totals.at[facet_id, :, tile_id // across, tile_id % across].add(result)
        return (totals, None)
    facet_image, _ = lax.scan(add_block, facet_image, (vis_flat, uv_flat, band_of, facet_flat, tile_flat))
    return facet_image.transpose(0, 1, 2, 4, 3, 5).reshape(FACETS, 2, FROWS, FCOLS)
```

```python
import jax
import jax.numpy as jnp
from jax import lax
from jax.experimental import pallas as pl
from jax.experimental.pallas import tpu as pltpu
from jax.sharding import PartitionSpec as P

TILE = 128
FCOLS = 2048
FROWS = 512
CAP = 2
CH = 16
NV = 64
ROWS = 32
HALF_P = ROWS // 2
HALF_Q = TILE // 2
COLS = FCOLS // TILE
PER = 40
GROUP = 2

SIN = (
    6.28318530472, -41.3417013429, 81.6051561334, -76.7017195864, 41.9691302047, -14.1604742051
)
COS = (
    0.999999999208, -19.7392080649, 64.9392827706, -85.4506731816, 60.0909654249, -24.6453426591
)

PHI_C, PHI_S, THETA_C, THETA_S, AMP_A, AMP_B, AMP_NA, AMP_NB, WEIGHT, STEP = (
    0, 16, 32, 48, 64, 65, 66, 67, 68, 69
)
QUANTITIES = 70


def horner(coefficients, x):
    total = jnp.full_like(x, coefficients[-1])
    for c in coefficients[-2::-1]:
        total = total * x + c
    return total


def sincos_quarter(x):
    square = x * x
    return x * horner(SIN, square), horner(COS, square)


def harmonics(cycles):
    s0, c0 = sincos_quarter(cycles * 0.5)
    double = c0 * c0 * 2.0 - 1.0
    sine = c0 * s0 * 2.0
    c1 = double * c0 - sine * s0
    s1 = sine * c0 + double * s0
    twice = double * double * 4.0 - 2.0
    cosines, sines = [c1, c0, c0, c1], [-s1, -s0, s0, s1]
    for j in range(4, 18):
        cosines.append(twice * cosines[j - 2] - cosines[j - 4])
        sines.append(twice * sines[j - 2] - sines[j - 4])
    return cosines[2:], sines[2:]


def prepare(code, live, base_row, base_col, vis_ref, u_ref, v_ref, f_ref, keep):
    slot = code // COLS
    column = code % COLS
    ratio = f_ref[slot // 32]
    fu = ratio * u_ref[pl.ds(slot, 1), :]
    fv = ratio * v_ref[pl.ds(slot, 1), :]
    col_centre = base_col + (column * TILE).astype(jnp.float32)
    x = fu * base_row
    y = fv * col_centre
    z = (x - jnp.round(x)) + (y - jnp.round(y))
    z = z - jnp.round(z)
    sh, ch = sincos_quarter(z * 0.5)
    sine = sh * ch * 2.0
    cosine = 1.0 - sh * sh * 2.0
    vis = vis_ref[slot // CAP, pl.ds(pl.multiple_of((slot % CAP) * 16, 16), 16), :].astype(jnp.float32)
    re = vis[:8] * live
    im = vis[8:] * live
    amp_a = re * cosine - im * sine
    amp_b = re * sine + im * cosine

    def put(quantity, value):
        keep[quantity * 8 : quantity * 8 + 8, :] = value

    phi_c, phi_s = harmonics(fv)
    theta_c, theta_s = harmonics(fu)
    for j in range(16):
        put(PHI_C + j, phi_c[j])
        put(PHI_S + j, phi_s[j])
        put(THETA_C + j, theta_c[j])
        put(THETA_S + j, theta_s[j])
    put(AMP_A, amp_a)
    put(AMP_B, amp_b)
    put(AMP_NA, -amp_a)
    put(AMP_NB, -amp_b)
    put(WEIGHT, (ratio - 1.0) * 10.0)
    put(STEP, (phi_c[7] * phi_c[0] - phi_s[7] * phi_s[0]) * 2.0)


def factors(keep, left, right):
    for part in range(8):
        lanes = slice(part * 128, part * 128 + 128)

        def eight(quantity, keep=keep, part=part):
            return keep[pl.ds(quantity * 8 + part, 8, stride=8), :]

        def one(quantity, keep=keep, part=part):
            return jnp.broadcast_to(keep[pl.ds(quantity * 8 + part, 1), :], (8, 128))

        weight = one(WEIGHT)
        theta_c = [eight(THETA_C), eight(THETA_C + 8)]
        theta_s = [eight(THETA_S), eight(THETA_S + 8)]
        kinds = ((AMP_A, theta_c), (AMP_NB, theta_s), (AMP_NA, theta_s), (AMP_NB, theta_c))
        for kind, (amp, theta) in enumerate(kinds):
            gain = one(amp)
            plain = [gain * theta[0], gain * theta[1]]
            scaled = [weight * plain[0], weight * plain[1]]
            for t, pair in enumerate((plain, scaled)):
                row = (kind * 2 + t) * 16
                left[row : row + 16, lanes] = jnp.concatenate(pair, axis=0).astype(jnp.bfloat16)
        step = one(STEP)
        for first, row in ((PHI_C, 0), (PHI_S, HALF_Q)):
            run = [eight(first), eight(first + 8)]
            for j in range(2, 8):
                run.append(step * run[j - 1] - run[j - 2])
            for j in range(0, 8, 2):
                right[row + j * 8 : row + j * 8 + 16, lanes] = jnp.concatenate(
                    run[j : j + 2], axis=0
                ).astype(jnp.bfloat16)


NT = (((1,), (1,)), ((), ()))


def gridder(list_ref, place_ref, vis_ref, u_ref, v_ref, f_ref, out_ref, acc, keeps, lefts, rights):
    acc[...] = jnp.zeros_like(acc)
    count = list_ref[512]
    base_row = place_ref[0]
    base_col = place_ref[1]

    def step(i, carry):
        for g in range(GROUP):
            at = i * GROUP + g
            code = list_ref[at]
            live = jnp.where(at < count, 1.0 / 32.0, 0.0)
            prepare(code, live, base_row, base_col, vis_ref, u_ref, v_ref, f_ref, keeps.at[g])
            factors(keeps.at[g], lefts.at[g], rights.at[g])
        for g in range(GROUP):
            code = list_ref[i * GROUP + g]
            column = code % COLS
            for half in range(2):
                rows = slice(half * 64, half * 64 + 64)
                acc[column, rows, :] += lax.dot_general(
                    lefts[g, rows, :], rights[g, rows, :], NT, preferred_element_type=jnp.float32
                )
        return carry

    lax.fori_loop(0, (count + GROUP - 1) // GROUP, step, 0)

    def iota(shape, dim):
        return lax.broadcasted_iota(jnp.int32, shape, dim)

    mirror = (iota((64, 128), 0) == 63 - iota((64, 128), 1)).astype(jnp.float32)
    shift = (iota((64, 128), 0) + 64 == iota((64, 128), 1)).astype(jnp.float32)
    turn = (iota((16, 16), 0) == 15 - iota((16, 16), 1)).astype(jnp.float32)

    def exact(a, b):
        return jnp.dot(a, b, precision=lax.Precision.HIGHEST, preferred_element_type=jnp.float32)

    for c in range(COLS):
        ee, oe, oo, eo = (acc[c, k * 32 : k * 32 + 32, :] for k in range(4))
        upper_even, upper_odd = ee + oe, oo + eo
        lower_even, lower_odd = ee - oe, eo - oo
        upper = exact(upper_even - upper_odd, mirror) + exact(upper_even + upper_odd, shift)
        lower = exact(lower_even - lower_odd, mirror) + exact(lower_even + lower_odd, shift)
        lanes = slice(c * 128, c * 128 + 128)
        for t in range(2):
            out_ref[t, 16:32, lanes] = upper[t * 16 : t * 16 + 16]
            out_ref[t, 0:16, lanes] = exact(turn, lower[t * 16 : t * 16 + 16])


def split_bf16(x):
    high = lax.reduce_precision(x, 8, 7)
    rest = x - high
    middle = lax.reduce_precision(rest, 8, 7)
    return [part.astype(jnp.bfloat16) for part in (high, middle, rest - middle)]


def shards(visibilities, uv_coords, freq_ratio, target_facet, tile_index):
    facets = lax.axis_size("facet")
    bands = lax.axis_size("band")
    my_facet = lax.axis_index("facet")
    my_band = lax.axis_index("band")
    targets = target_facet[0, :, 0]
    blocks = targets.shape[0]
    order = jnp.arange(blocks, dtype=jnp.int32)

    alike = (targets[:, None] == targets[None, :]) & (order[None, :] < order[:, None])
    rank = jnp.sum(alike.astype(jnp.int32), axis=1)
    slots = jnp.arange(facets * CAP, dtype=jnp.int32)
    chosen = (targets * CAP + rank)[None, :] == slots[:, None]
    pick = chosen.astype(jnp.bfloat16)

    def picked(rows):
        return jnp.dot(pick, rows, preferred_element_type=jnp.float32).astype(jnp.bfloat16)

    sent_vis = picked(visibilities[0].reshape(blocks, 2 * CH * NV)).reshape(facets, CAP * 16, 128)
    sent_uv = picked(uv_coords[0].reshape(blocks, 2 * NV)).reshape(facets, CAP, 128)
    sent_tile = jnp.sum(jnp.where(chosen, tile_index[0][None, :] + 1, 0), axis=1)
    sent_tile = sent_tile.astype(jnp.bfloat16).reshape(facets, 1, CAP)
    ratio_row = jnp.concatenate(split_bf16(freq_ratio), axis=1)[None]
    numbers = jnp.concatenate(
        [
            sent_tile,
            jnp.broadcast_to(ratio_row, (facets, 1, 3 * CH)),
            jnp.zeros((facets, 1, 128 - CAP - 3 * CH), jnp.bfloat16),
        ],
        axis=2,
    )
    pad = jnp.zeros((facets, PER - CAP * 17 - 1, 128), jnp.bfloat16)
    send = jnp.concatenate([sent_vis, sent_uv, numbers, pad], axis=1)

    mine = lax.all_to_all(send, "facet", 0, 0, tiled=True)
    held = lax.all_gather(mine, "band", axis=0, tiled=True)

    aux = held[:, 32:35, :].astype(jnp.float32)
    uv = aux[:, 0:2, :].reshape(-1, 128)
    u_rows = jnp.concatenate([uv[:, :NV], uv[:, :NV]], axis=1)
    v_rows = jnp.concatenate([uv[:, NV:], uv[:, NV:]], axis=1)
    tiles = aux[:, 2, :CAP].reshape(-1).astype(jnp.int32) - 1
    parts = aux[:: facets, 2, CAP : CAP + 3 * CH].reshape(bands, 3, CH)
    ratio = (parts[:, 0] + parts[:, 1]) + parts[:, 2]
    ratio = jnp.repeat(ratio.reshape(bands, 8, 2), NV, axis=2)

    total = tiles.shape[0]
    index = jnp.arange(total, dtype=jnp.int32)
    my_row = my_band // (bands // (FROWS // TILE))
    match = (tiles >= 0) & (tiles // COLS == my_row)
    before = jnp.sum((match[None, :] & (index[None, :] < index[:, None])).astype(jnp.int32), axis=1)
    codes = index * COLS + tiles % COLS
    goes = match[None, :] & (before[None, :] == index[:, None])
    work = jnp.sum(jnp.where(goes, codes[None, :], 0), axis=1)
    count = jnp.sum(match.astype(jnp.int32))
    work = jnp.concatenate([work, count[None], jnp.zeros((7,), jnp.int32)])
    place = jnp.stack(
        [
            FROWS * (my_facet % 4 - 2) + ROWS * my_band,
            FCOLS * (my_facet // 4 % 4 - 2),
        ]
    ).astype(jnp.float32) + jnp.array([(ROWS - 1) / 2, (TILE - 1) / 2], jnp.float32)

    smem = pl.BlockSpec(memory_space=pltpu.SMEM)
    vmem = pl.BlockSpec(memory_space=pltpu.VMEM)
    image = pl.pallas_call(
        gridder,
        out_shape=jax.ShapeDtypeStruct((2, ROWS, FCOLS), jnp.float32),
        in_specs=[smem, smem, vmem, vmem, vmem, vmem],
        out_specs=vmem,
        scratch_shapes=[
            pltpu.VMEM((COLS, 128, 64), jnp.float32),
            pltpu.VMEM((GROUP, QUANTITIES * 8, 128), jnp.float32),
            pltpu.VMEM((GROUP, 128, CH * NV), jnp.bfloat16),
            pltpu.VMEM((GROUP, 128, CH * NV), jnp.bfloat16),
        ],
        compiler_params=pltpu.CompilerParams(vmem_limit_bytes=40 * 1024 * 1024),
        name="gridder",
    )(work, place, held, u_rows, v_rows, ratio)
    return image[None]


def solution(mesh):
    return jax.shard_map(
        shards,
        mesh=mesh,
        in_specs=(
            P("band", "facet", None, None),
            P("band", "facet", None, None),
            P("band", None),
            P("band", "facet", None),
            P("band", "facet"),
        ),
        out_specs=P("facet", None, "band", None),
        check_vma=False,
    )
```

```python
import functools

import jax
import jax.numpy as jnp
from jax import lax
from jax.experimental import pallas as pl
from jax.experimental.pallas import tpu as pltpu
from jax.sharding import PartitionSpec as P

TILE = 128
FCOLS = 2048
FROWS = 512
CAP = 2
CH = 16
NV = 64
ROWS = 32
HALF_P = ROWS // 2
HALF_Q = TILE // 2
COLS = FCOLS // TILE
PER = 40
GROUP = 4
DEEP = 2

SIN = (
    6.28318530472, -41.3417013429, 81.6051561334, -76.7017195864, 41.9691302047, -14.1604742051
)
COS = (
    0.999999999208, -19.7392080649, 64.9392827706, -85.4506731816, 60.0909654249, -24.6453426591
)

PHI_C, PHI_S, THETA_C, THETA_S, AMP_A, AMP_B, AMP_NA, AMP_NB, WEIGHT, STEP = (
    0, 16, 32, 48, 64, 65, 66, 67, 68, 69
)
QUANTITIES = 70


def horner(coefficients, x):
    total = jnp.full_like(x, coefficients[-1])
    for c in coefficients[-2::-1]:
        total = total * x + c
    return total


def sincos_quarter(x):
    square = x * x
    return x * horner(SIN, square), horner(COS, square)


def harmonics(cycles):
    s0, c0 = sincos_quarter(cycles * 0.5)
    double = c0 * c0 * 2.0 - 1.0
    sine = c0 * s0 * 2.0
    c1 = double * c0 - sine * s0
    s1 = sine * c0 + double * s0
    twice = double * double * 4.0 - 2.0
    cosines, sines = [c1, c0, c0, c1], [-s1, -s0, s0, s1]
    for j in range(4, 18):
        cosines.append(twice * cosines[j - 2] - cosines[j - 4])
        sines.append(twice * sines[j - 2] - sines[j - 4])
    return cosines[2:], sines[2:]


def prepare(code, live, base_row, base_col, vis_ref, u_ref, v_ref, f_ref, keep):
    slot = code // COLS
    column = code % COLS
    ratio = f_ref[slot // 32]
    fu = ratio * u_ref[pl.ds(slot, 1), :]
    fv = ratio * v_ref[pl.ds(slot, 1), :]
    col_centre = base_col + (column * TILE).astype(jnp.float32)
    x = fu * base_row
    y = fv * col_centre
    z = (x - jnp.round(x)) + (y - jnp.round(y))
    z = z - jnp.round(z)
    sh, ch = sincos_quarter(z * 0.5)
    sine = sh * ch * 2.0
    cosine = 1.0 - sh * sh * 2.0
    vis = vis_ref[slot // CAP, pl.ds(pl.multiple_of((slot % CAP) * 16, 16), 16), :].astype(jnp.float32)
    re = vis[:8] * live
    im = vis[8:] * live
    amp_a = re * cosine - im * sine
    amp_b = re * sine + im * cosine

    def put(quantity, value):
        keep[quantity * 8 : quantity * 8 + 8, :] = value

    phi_c, phi_s = harmonics(fv)
    theta_c, theta_s = harmonics(fu)
    for j in range(16):
        put(PHI_C + j, phi_c[j])
        put(PHI_S + j, phi_s[j])
        put(THETA_C + j, theta_c[j])
        put(THETA_S + j, theta_s[j])
    put(AMP_A, amp_a)
    put(AMP_B, amp_b)
    put(AMP_NA, -amp_a)
    put(AMP_NB, -amp_b)
    put(WEIGHT, (ratio - 1.0) * 10.0)
    put(STEP, (phi_c[7] * phi_c[0] - phi_s[7] * phi_s[0]) * 2.0)


def factors(keep, part):
    def eight(quantity):
        return keep[pl.ds(quantity * 8 + part, 8, stride=8), :]

    def one(quantity):
        return jnp.broadcast_to(keep[pl.ds(quantity * 8 + part, 1), :], (8, 128))

    weight = one(WEIGHT)
    theta_c = [eight(THETA_C), eight(THETA_C + 8)]
    theta_s = [eight(THETA_S), eight(THETA_S + 8)]
    kinds = ((AMP_A, theta_c), (AMP_NB, theta_s), (AMP_NA, theta_s), (AMP_NB, theta_c))
    left = []
    for amp, theta in kinds:
        gain = one(amp)
        plain = [gain * theta[0], gain * theta[1]]
        left += plain + [weight * plain[0], weight * plain[1]]
    step = one(STEP)
    right = []
    for first in (PHI_C, PHI_S):
        run = [eight(first), eight(first + 8)]
        for j in range(2, 8):
            run.append(step * run[j - 1] - run[j - 2])
        right += run
    return (
        jnp.concatenate(left, axis=0).astype(jnp.bfloat16),
        jnp.concatenate(right, axis=0).astype(jnp.bfloat16),
    )


NT = (((1,), (1,)), ((), ()))


def product(keep):
    sums = [None, None]
    for part in range(0, 8, DEEP):
        made = [factors(keep, part + k) for k in range(DEEP)]
        left = jnp.concatenate([m[0] for m in made], axis=1)
        right = jnp.concatenate([m[1] for m in made], axis=1)
        for half in range(2):
            rows = slice(half * 64, half * 64 + 64)
            term = lax.dot_general(left[rows], right[rows], NT, preferred_element_type=jnp.float32)
            sums[half] = term if sums[half] is None else sums[half] + term
    return sums


def unfold_image(acc, out_ref):
    lane = lax.broadcasted_iota(jnp.int32, (8, 128), 1)
    spread = jnp.where(lane < 64, 63 - lane, lane - 64)
    sign = jnp.where(lane < 64, -1.0, 1.0)
    turn = 7 - lax.broadcasted_iota(jnp.int32, (8, 128), 0)

    def unfold(even, odd):
        even = jnp.concatenate([even, even], axis=1)
        odd = jnp.concatenate([odd, odd], axis=1)
        even = jnp.take_along_axis(even, spread, axis=1)
        return even + sign * jnp.take_along_axis(odd, spread, axis=1)

    def column(c, carry):
        lanes = pl.ds(pl.multiple_of(c * 128, 128), 128)
        for t in range(2):
            for j in range(2):
                at = t * 16 + j * 8
                ee, oe, oo, eo = (acc[c, k * 32 + at : k * 32 + at + 8, :] for k in range(4))
                out_ref[t, 16 + j * 8 : 24 + j * 8, lanes] = unfold(ee + oe, oo + eo)
                lower = unfold(ee - oe, eo - oo)
                out_ref[t, 8 - j * 8 : 16 - j * 8, lanes] = jnp.take_along_axis(lower, turn, axis=0)
        return carry

    lax.fori_loop(0, COLS, column, 0)


def gridder(first, last, list_ref, place_ref, vis_ref, u_ref, v_ref, f_ref, *rest):
    rest = list(rest)
    before = None if first else rest.pop(0)
    out_ref = rest.pop(0)
    acc = rest.pop(0) if last else out_ref
    keeps = rest.pop(0)
    acc[...] = jnp.zeros_like(acc) if first else before[...]
    count = list_ref[list_ref.shape[0] - 1]
    base_row = place_ref[0]
    base_col = place_ref[1]

    def step(i, carry):
        for g in range(GROUP):
            at = i * GROUP + g
            live = jnp.where(at < count, 1.0 / 32.0, 0.0)
            prepare(list_ref[at], live, base_row, base_col, vis_ref, u_ref, v_ref, f_ref, keeps.at[g])
        sums = [product(keeps.at[g]) for g in range(GROUP)]
        for g in range(GROUP):
            column = list_ref[i * GROUP + g] % COLS
            for half in range(2):
                acc[column, half * 64 : half * 64 + 64, :] += sums[g][half]
        return carry

    lax.fori_loop(0, (count + GROUP - 1) // GROUP, step, 0)
    if last:
        unfold_image(acc, out_ref)


def work_list(held, my_row):
    aux = held[:, 32:35, :].astype(jnp.float32)
    uv = aux[:, 0:2, :].reshape(-1, 128)
    u_rows = jnp.concatenate([uv[:, :NV], uv[:, :NV]], axis=1)
    v_rows = jnp.concatenate([uv[:, NV:], uv[:, NV:]], axis=1)
    tiles = aux[:, 2, :CAP].reshape(-1).astype(jnp.int32) - 1
    sources = 16
    bands = held.shape[0] // sources
    parts = aux[::sources, 2, CAP : CAP + 3 * CH].reshape(bands, 3, CH)
    ratio = (parts[:, 0] + parts[:, 1]) + parts[:, 2]
    ratio = jnp.repeat(ratio.reshape(bands, 8, 2), NV, axis=2)
    total = tiles.shape[0]
    index = jnp.arange(total, dtype=jnp.int32)
    match = (tiles >= 0) & (tiles // COLS == my_row)
    before = jnp.sum((match[None, :] & (index[None, :] < index[:, None])).astype(jnp.int32), axis=1)
    codes = index * COLS + tiles % COLS
    size = total + 16
    at = jnp.arange(size, dtype=jnp.int32)
    goes = match[None, :] & (before[None, :] == at[:, None])
    work = jnp.sum(jnp.where(goes, codes[None, :], 0), axis=1)
    count = jnp.sum(match.astype(jnp.int32))
    work = jnp.where(at == size - 1, count, work)
    return work, u_rows, v_rows, ratio


def grid_part(pieces, my_row, place, before, last):
    held = jnp.concatenate(pieces, axis=0) if len(pieces) > 1 else pieces[0]
    work, u_rows, v_rows, ratio = work_list(held, my_row)
    smem = pl.BlockSpec(memory_space=pltpu.SMEM)
    vmem = pl.BlockSpec(memory_space=pltpu.VMEM)
    first = before is None
    sums = (COLS, 128, 64)
    operands = [work, place, held, u_rows, v_rows, ratio] + ([] if first else [before])
    scratch = [pltpu.VMEM((GROUP, QUANTITIES * 8, 128), jnp.float32)]
    expected = held.shape[0] * CAP // 4
    return pl.pallas_call(
        functools.partial(gridder, first, last),
        out_shape=jax.ShapeDtypeStruct((2, ROWS, FCOLS) if last else sums, jnp.float32),
        in_specs=[smem, smem] + [vmem] * (len(operands) - 2),
        out_specs=vmem,
        scratch_shapes=([pltpu.VMEM(sums, jnp.float32)] if last else []) + scratch,
        compiler_params=pltpu.CompilerParams(vmem_limit_bytes=32 * 1024 * 1024),
        cost_estimate=pl.CostEstimate(
            flops=expected * 200_000_000, bytes_accessed=held.size * 2, transcendentals=0
        ),
        name="gridder",
    )(*operands)


def split_bf16(x):
    high = lax.reduce_precision(x, 8, 7)
    rest = x - high
    middle = lax.reduce_precision(rest, 8, 7)
    return [part.astype(jnp.bfloat16) for part in (high, middle, rest - middle)]


def shards(visibilities, uv_coords, freq_ratio, target_facet, tile_index):
    facets = lax.axis_size("facet")
    bands = lax.axis_size("band")
    my_facet = lax.axis_index("facet")
    my_band = lax.axis_index("band")
    targets = target_facet[0, :, 0]
    blocks = targets.shape[0]
    order = jnp.arange(blocks, dtype=jnp.int32)

    alike = (targets[:, None] == targets[None, :]) & (order[None, :] < order[:, None])
    rank = jnp.sum(alike.astype(jnp.int32), axis=1)
    slots = jnp.arange(facets * CAP, dtype=jnp.int32)
    chosen = (targets * CAP + rank)[None, :] == slots[:, None]
    pick = chosen.astype(jnp.bfloat16)

    def picked(rows):
        return jnp.dot(pick, rows, preferred_element_type=jnp.float32).astype(jnp.bfloat16)

    sent_vis = picked(visibilities[0].reshape(blocks, 2 * CH * NV)).reshape(facets, CAP * 16, 128)
    sent_uv = picked(uv_coords[0].reshape(blocks, 2 * NV)).reshape(facets, CAP, 128)
    sent_tile = jnp.sum(jnp.where(chosen, tile_index[0][None, :] + 1, 0), axis=1)
    sent_tile = sent_tile.astype(jnp.bfloat16).reshape(facets, 1, CAP)
    ratio_row = jnp.concatenate(split_bf16(freq_ratio), axis=1)[None]
    numbers = jnp.concatenate(
        [
            sent_tile,
            jnp.broadcast_to(ratio_row, (facets, 1, 3 * CH)),
            jnp.zeros((facets, 1, 128 - CAP - 3 * CH), jnp.bfloat16),
        ],
        axis=2,
    )
    pad = jnp.zeros((facets, PER - CAP * 17 - 1, 128), jnp.bfloat16)
    send = jnp.concatenate([sent_vis, sent_uv, numbers, pad], axis=1)

    mine = lax.all_to_all(send, "facet", 0, 0, tiled=True)
    my_row = my_band // (bands // (FROWS // TILE))
    place = jnp.stack(
        [
            FROWS * (my_facet % 4 - 2) + ROWS * my_band,
            FCOLS * (my_facet // 4 % 4 - 2),
        ]
    ).astype(jnp.float32) + jnp.array([(ROWS - 1) / 2, (TILE - 1) / 2], jnp.float32)

    def over_y(x):
        return lax.ppermute(x, "band", [(i, i ^ 8) for i in range(bands)])

    def over_core(x):
        return lax.ppermute(x, "band", [(i, i ^ 1) for i in range(bands)])

    def over_x(x, d):
        ring = [(i, i // 8 * 8 + (i % 8 // 2 + d) % 4 * 2 + i % 2) for i in range(bands)]
        return lax.ppermute(x, "band", ring)

    half = facets // 2
    other = over_core(mine)
    from_y, from_up, from_down = over_y(mine), over_x(mine, 1), over_x(mine, 3)
    near = jnp.concatenate([from_y, from_up, from_down], axis=0)
    near_other = over_core(near)
    far_x = jnp.concatenate([over_x(from_up[:half], 1), over_x(from_down[half:], 3)], axis=0)
    far = jnp.concatenate(
        [over_y(jnp.concatenate([from_up, from_down], axis=0)), far_x, over_y(far_x)], axis=0
    )
    far_other = over_core(far)

    image = grid_part([mine, other], my_row, place, None, False)
    image = grid_part([near, near_other], my_row, place, image, False)
    image = grid_part([far, far_other], my_row, place, image, True)
    return image[None]


def solution(mesh):
    return jax.shard_map(
        shards,
        mesh=mesh,
        in_specs=(
            P("band", "facet", None, None),
            P("band", "facet", None, None),
            P("band", None),
            P("band", "facet", None),
            P("band", "facet"),
        ),
        out_specs=P("facet", None, "band", None),
        check_vma=False,
    )
```

```python
import functools

import jax
import jax.numpy as jnp
from jax import lax
from jax.experimental import pallas as pl
from jax.experimental.pallas import tpu as pltpu
from jax.sharding import PartitionSpec as P

TILE = 128
FCOLS = 2048
FROWS = 512
CAP = 2
CH = 16
NV = 64
ROWS = 64
HALF_P = ROWS // 2
HALF_Q = TILE // 2
COLS = FCOLS // TILE
PER = 40
GROUP = 4
RATIO_AT = 3
DEEP = 2

SIN = (
    6.28318530472, -41.3417013429, 81.6051561334, -76.7017195864, 41.9691302047, -14.1604742051
)
COS = (
    0.999999999208, -19.7392080649, 64.9392827706, -85.4506731816, 60.0909654249, -24.6453426591
)

PHI_C, PHI_S, THETA_C, THETA_S, AMP_A, AMP_B, AMP_NA, AMP_NB, WEIGHT, STEP, THETA_STEP = (
    0, 16, 32, 48, 64, 65, 66, 67, 68, 69, 70
)
QUANTITIES = 71


def horner(coefficients, x):
    total = jnp.full_like(x, coefficients[-1])
    for c in coefficients[-2::-1]:
        total = total * x + c
    return total


def sincos_quarter(x):
    square = x * x
    return x * horner(SIN, square), horner(COS, square)


def harmonics(cycles):
    s0, c0 = sincos_quarter(cycles * 0.5)
    double = c0 * c0 * 2.0 - 1.0
    sine = c0 * s0 * 2.0
    c1 = double * c0 - sine * s0
    s1 = sine * c0 + double * s0
    twice = double * double * 4.0 - 2.0
    cosines, sines = [c1, c0, c0, c1], [-s1, -s0, s0, s1]
    for j in range(4, 18):
        cosines.append(twice * cosines[j - 2] - cosines[j - 4])
        sines.append(twice * sines[j - 2] - sines[j - 4])
    return cosines[2:], sines[2:]


def prepare(codes, lives, base_row, base_col, vis_ref, aux_ref, keeps):
    lane = lax.broadcasted_iota(jnp.int32, (8, 128), 1)
    spread = lax.broadcasted_iota(jnp.int32, (8, 128), 0) * 2 + lane // NV
    ratios, uvs, res, ims, centres = [], [], [], [], []
    for code, live in zip(codes, lives):
        slot = code // COLS
        source = slot // CAP
        row = jnp.sum(aux_ref[source, RATIO_AT : RATIO_AT + 3, :], axis=0, keepdims=True)
        ratios.append(jnp.broadcast_to(row, (8, 128)))
        uvs.append(jnp.broadcast_to(aux_ref[source, pl.ds(slot % CAP, 1), :], (8, 128)))
        first = pl.multiple_of((slot % CAP) * 16, 16)
        vis = vis_ref[source, pl.ds(first, 16), :].astype(jnp.float32)
        res.append(vis[:8] * live)
        ims.append(vis[8:] * live)
        centre = base_col + ((code % COLS) * TILE).astype(jnp.float32)
        centres.append(jnp.full((8, 128), centre, jnp.float32))

    def stack(rows):
        return jnp.concatenate(rows, axis=0)

    ratio = stack([jnp.take_along_axis(r, spread, axis=1) for r in ratios])
    uv = stack(uvs)
    vu = stack([pltpu.roll(x, NV, 1) for x in uvs])
    low = stack([lane] * len(codes)) < NV
    fu = ratio * jnp.where(low, uv, vu)
    fv = ratio * jnp.where(low, vu, uv)
    x = fu * base_row
    y = fv * stack(centres)
    z = (x - jnp.round(x)) + (y - jnp.round(y))
    z = z - jnp.round(z)
    sh, ch = sincos_quarter(z * 0.5)
    sine = sh * ch * 2.0
    cosine = 1.0 - sh * sh * 2.0
    re, im = stack(res), stack(ims)
    amp_a = re * cosine - im * sine
    amp_b = re * sine + im * cosine

    def put(quantity, value):
        for g in range(len(codes)):
            keeps[g, quantity * 8 : quantity * 8 + 8, :] = value[g * 8 : g * 8 + 8]

    put(AMP_A, amp_a)
    put(AMP_B, amp_b)
    put(AMP_NA, -amp_a)
    put(AMP_NB, -amp_b)
    put(WEIGHT, (ratio - 1.0) * 10.0)
    theta_c, theta_s = harmonics(fu)
    phi_c, phi_s = harmonics(fv)
    for j in range(16):
        put(THETA_C + j, theta_c[j])
        put(THETA_S + j, theta_s[j])
        put(PHI_C + j, phi_c[j])
        put(PHI_S + j, phi_s[j])
    put(STEP, (phi_c[7] * phi_c[0] - phi_s[7] * phi_s[0]) * 2.0)
    put(THETA_STEP, (theta_c[7] * theta_c[0] - theta_s[7] * theta_s[0]) * 2.0)


def factors(keep, part):
    def eight(quantity):
        return keep[pl.ds(quantity * 8 + part, 8, stride=8), :]

    def one(quantity):
        return jnp.broadcast_to(keep[pl.ds(quantity * 8 + part, 1), :], (8, 128))

    def ladder(first, step, size):
        run = [eight(first), eight(first + 8)]
        for j in range(2, size):
            run.append(step * run[j - 1] - run[j - 2])
        return run

    weight = one(WEIGHT)
    theta_step = one(THETA_STEP)
    theta_c = ladder(THETA_C, theta_step, HALF_P // 8)
    theta_s = ladder(THETA_S, theta_step, HALF_P // 8)
    kinds = ((AMP_A, theta_c), (AMP_NB, theta_s), (AMP_NA, theta_s), (AMP_NB, theta_c))
    left = []
    for amp, theta in kinds:
        gain = one(amp)
        plain = [gain * value for value in theta]
        left += plain + [weight * value for value in plain]
    step = one(STEP)
    right = ladder(PHI_C, step, HALF_Q // 8) + ladder(PHI_S, step, HALF_Q // 8)
    return (
        jnp.concatenate(left, axis=0).astype(jnp.bfloat16),
        jnp.concatenate(right, axis=0).astype(jnp.bfloat16),
    )


NT = (((1,), (1,)), ((), ()))


def product(keep):
    sums = [None, None]
    for part in range(0, 8, DEEP):
        made = [factors(keep, part + k) for k in range(DEEP)]
        left = jnp.concatenate([m[0] for m in made], axis=1)
        right = jnp.concatenate([m[1] for m in made], axis=1)
        for half in range(2):
            rows = slice(half * 2 * ROWS, half * 2 * ROWS + 2 * ROWS)
            cols = slice(half * HALF_Q, half * HALF_Q + HALF_Q)
            term = lax.dot_general(left[rows], right[cols], NT, preferred_element_type=jnp.float32)
            sums[half] = term if sums[half] is None else sums[half] + term
    return sums


def unfold_image(acc, lower_ref, upper_ref):
    lane = lax.broadcasted_iota(jnp.int32, (8, 128), 1)
    spread = jnp.where(lane < 64, 63 - lane, lane - 64)
    sign = jnp.where(lane < 64, -1.0, 1.0)
    turn = 7 - lax.broadcasted_iota(jnp.int32, (8, 128), 0)

    def unfold(even, odd):
        even = jnp.take_along_axis(even, spread, axis=1)
        return even + sign * jnp.take_along_axis(odd, spread, axis=1)

    def column(c, carry):
        lanes = pl.ds(pl.multiple_of(c * 128, 128), 128)
        for t in range(2):
            for j in range(HALF_P // 8):
                at = t * HALF_P + j * 8
                ee, oe, oo, eo = (acc[c, k * ROWS + at : k * ROWS + at + 8, :] for k in range(4))
                upper_ref[t, j * 8 : j * 8 + 8, lanes] = unfold(ee + oe, oo + eo)
                lower = unfold(ee - oe, eo - oo)
                to = HALF_P - 8 - j * 8
                lower_ref[t, to : to + 8, lanes] = jnp.take_along_axis(lower, turn, axis=0)
        return carry

    lax.fori_loop(0, COLS, column, 0)


def gridder(first, last, tile_ref, row_ref, place_ref, vis_ref, aux_ref, *rest):
    rest = list(rest)
    before = None if first else rest.pop(0)
    if last:
        own_ref, other_ref, acc = rest.pop(0), rest.pop(0), rest.pop(0)
    else:
        acc = rest.pop(0)
    keeps, work = rest
    acc[...] = jnp.zeros_like(acc) if first else before[...]
    my_row = row_ref[0]
    base_row = place_ref[0]
    base_col = place_ref[1]
    slots = tile_ref.shape[0]

    def visit(i, count):
        for k in range(8):
            slot = i * 8 + k
            tile = tile_ref[slot] - 1
            work[count] = slot * COLS + (tile & (COLS - 1))
            count = count + jnp.where((tile >> 4) == my_row, 1, 0)
        return count

    count = lax.fori_loop(0, slots // 8, visit, 0)
    for g in range(GROUP):
        work[count + g] = 0

    def step(i, carry):
        codes = [work[i * GROUP + g] for g in range(GROUP)]
        lives = [jnp.where(i * GROUP + g < count, 1.0 / 32.0, 0.0) for g in range(GROUP)]
        prepare(codes, lives, base_row, base_col, vis_ref, aux_ref, keeps)
        sums = [product(keeps.at[g]) for g in range(GROUP)]
        for g in range(GROUP):
            column = work[i * GROUP + g] % COLS
            for half in range(2):
                acc[column, half * 2 * ROWS : (half + 1) * 2 * ROWS, :HALF_Q] += sums[g][half]
        return carry

    lax.fori_loop(0, (count + GROUP - 1) // GROUP, step, 0)
    if last:

        @pl.when(row_ref[1] == 0)
        def _():
            unfold_image(acc, own_ref, other_ref)

        @pl.when(row_ref[1] != 0)
        def _():
            unfold_image(acc, other_ref, own_ref)


def grid_part(held, my_row, place, before, last):
    aux = held[:, CAP * 16 : PER, :].astype(jnp.float32)
    tiles = aux[:, 2, :CAP].astype(jnp.int32).reshape(-1)
    smem = pl.BlockSpec(memory_space=pltpu.SMEM)
    vmem = pl.BlockSpec(memory_space=pltpu.VMEM)
    first = before is None
    sums = jax.ShapeDtypeStruct((COLS, 4 * ROWS, TILE), jnp.float32)
    rows = jax.ShapeDtypeStruct((2, HALF_P, FCOLS), jnp.float32)
    operands = [tiles, my_row, place, held, aux] + ([] if first else [before])
    scratch = [
        pltpu.VMEM((GROUP, QUANTITIES * 8, 128), jnp.float32),
        pltpu.SMEM((tiles.shape[0] + GROUP + 4,), jnp.int32),
    ]
    expected = held.shape[0] * CAP // 4
    return pl.pallas_call(
        functools.partial(gridder, first, last),
        out_shape=(rows, rows) if last else sums,
        in_specs=[smem, smem, smem] + [vmem] * (len(operands) - 3),
        out_specs=(vmem, vmem) if last else vmem,
        scratch_shapes=([pltpu.VMEM(sums.shape, sums.dtype)] if last else []) + scratch,
        compiler_params=pltpu.CompilerParams(vmem_limit_bytes=32 * 1024 * 1024),
        cost_estimate=pl.CostEstimate(
            flops=expected * 200_000_000, bytes_accessed=held.size * 2, transcendentals=0
        ),
        name="gridder",
    )(*operands)


def split_bf16(x):
    high = lax.reduce_precision(x, 8, 7)
    rest = x - high
    middle = lax.reduce_precision(rest, 8, 7)
    return [part.astype(jnp.bfloat16) for part in (high, middle, rest - middle)]


def shards(visibilities, uv_coords, freq_ratio, target_facet, tile_index):
    facets = lax.axis_size("facet")
    bands = lax.axis_size("band")
    my_facet = lax.axis_index("facet")
    my_band = lax.axis_index("band")
    targets = target_facet[0, :, 0]
    blocks = targets.shape[0]
    order = jnp.arange(blocks, dtype=jnp.int32)

    alike = (targets[:, None] == targets[None, :]) & (order[None, :] < order[:, None])
    rank = jnp.sum(alike.astype(jnp.int32), axis=1)
    slots = jnp.arange(facets * CAP, dtype=jnp.int32)
    chosen = (targets * CAP + rank)[None, :] == slots[:, None]
    pick = chosen.astype(jnp.bfloat16)

    def picked(rows):
        return jnp.dot(pick, rows, preferred_element_type=jnp.float32).astype(jnp.bfloat16)

    sent_vis = picked(visibilities[0].reshape(blocks, 2 * CH * NV)).reshape(facets, CAP * 16, 128)
    sent_uv = picked(uv_coords[0].reshape(blocks, 2 * NV)).reshape(facets, CAP, 128)
    sent_tile = jnp.sum(jnp.where(chosen, tile_index[0][None, :] + 1, 0), axis=1)
    sent_tile = sent_tile.astype(jnp.bfloat16).reshape(facets, 1, CAP)
    tile_row = jnp.pad(sent_tile, ((0, 0), (0, 0), (0, 128 - CAP)))
    ratio_rows = jnp.pad(jnp.concatenate(split_bf16(freq_ratio), axis=0), ((0, 0), (0, 128 - CH)))
    ratio_rows = jnp.broadcast_to(ratio_rows[None], (facets, 3, 128))
    pad = jnp.zeros((facets, PER - CAP * 17 - 4, 128), jnp.bfloat16)
    send = jnp.concatenate([sent_vis, sent_uv, tile_row, ratio_rows, pad], axis=1)

    mine = lax.all_to_all(send, "facet", 0, 0, tiled=True)
    tile_row = my_band // (bands // (FROWS // TILE))
    my_row = jnp.stack([tile_row, my_band % 2]).astype(jnp.int32)
    place = jnp.stack(
        [
            FROWS * (my_facet % 4 - 2) + ROWS * (my_band // 2),
            FCOLS * (my_facet // 4 % 4 - 2),
        ]
    ).astype(jnp.float32) + jnp.array([(ROWS - 1) / 2, (TILE - 1) / 2], jnp.float32)

    def over_y(x):
        return lax.ppermute(x, "band", [(i, i ^ 8) for i in range(bands)])

    def over_core(x):
        return lax.ppermute(x, "band", [(i, i ^ 1) for i in range(bands)])

    def over_x(x, d):
        ring = [(i, i // 8 * 8 + (i % 8 // 2 + d) % 4 * 2 + i % 2) for i in range(bands)]
        return lax.ppermute(x, "band", ring)

    half = facets // 2
    from_y, from_up, from_down = over_y(mine), over_x(mine, 1), over_x(mine, 3)
    sums = grid_part(mine, my_row, place, None, False)
    from_up, from_down, sums = lax.optimization_barrier((from_up, from_down, sums))
    sides = jnp.concatenate([from_up, from_down], axis=0)
    opposite = [over_x(from_up[:half], 1), over_x(from_down[half:], 3)]
    across = over_y(sides)
    sums = grid_part(jnp.concatenate([from_y, sides], axis=0), my_row, place, sums, False)
    far = jnp.concatenate(opposite, axis=0)
    far, across, sums = lax.optimization_barrier((far, across, sums))
    farthest = over_y(far)
    sums = grid_part(jnp.concatenate([across, far], axis=0), my_row, place, sums, False)
    own, other = grid_part(farthest, my_row, place, sums, True)
    return (own + over_core(other))[None]


def solution(mesh):
    return jax.shard_map(
        shards,
        mesh=mesh,
        in_specs=(
            P("band", "facet", None, None),
            P("band", "facet", None, None),
            P("band", None),
            P("band", "facet", None),
            P("band", "facet"),
        ),
        out_specs=P("facet", None, "band", None),
        check_vma=False,
    )
```

```python
import functools

import jax
import jax.numpy as jnp
from jax import lax
from jax.experimental import pallas as pl
from jax.experimental.pallas import tpu as pltpu
from jax.sharding import PartitionSpec as P

TILE = 128
FCOLS = 2048
FROWS = 512
CAP = 2
CH = 16
NV = 64
ROWS = 64
HALF_P = ROWS // 2
HALF_Q = TILE // 2
COLS = FCOLS // TILE
PER = 40
GROUP = 4
RATIO_AT = 3
DEEP = 2

SIN = (
    6.28318530472, -41.3417013429, 81.6051561334, -76.7017195864, 41.9691302047, -14.1604742051
)
COS = (
    0.999999999208, -19.7392080649, 64.9392827706, -85.4506731816, 60.0909654249, -24.6453426591
)

PHI_C, PHI_S, THETA_C, THETA_S, AMP_A, AMP_B, AMP_NA, AMP_NB, WEIGHT, STEP, THETA_STEP = (
    0, 16, 32, 48, 64, 65, 66, 67, 68, 69, 70
)
QUANTITIES = 71


def horner(coefficients, x):
    total = jnp.full_like(x, coefficients[-1])
    for c in coefficients[-2::-1]:
        total = total * x + c
    return total


def sincos_quarter(x):
    square = x * x
    return x * horner(SIN, square), horner(COS, square)


def harmonics(cycles):
    s0, c0 = sincos_quarter(cycles * 0.5)
    double = c0 * c0 * 2.0 - 1.0
    sine = c0 * s0 * 2.0
    c1 = double * c0 - sine * s0
    s1 = sine * c0 + double * s0
    twice = double * double * 4.0 - 2.0
    cosines, sines = [c1, c0, c0, c1], [-s1, -s0, s0, s1]
    for j in range(4, 18):
        cosines.append(twice * cosines[j - 2] - cosines[j - 4])
        sines.append(twice * sines[j - 2] - sines[j - 4])
    return cosines[2:], sines[2:]


def prepare(codes, lives, base_row, base_col, vis_ref, aux_ref, keeps):
    lane = lax.broadcasted_iota(jnp.int32, (8, 128), 1)
    spread = lax.broadcasted_iota(jnp.int32, (8, 128), 0) * 2 + lane // NV
    ratios, uvs, res, ims, centres = [], [], [], [], []
    for code, live in zip(codes, lives):
        slot = code // COLS
        source = slot // CAP
        row = jnp.sum(aux_ref[source, RATIO_AT : RATIO_AT + 3, :], axis=0, keepdims=True)
        ratios.append(jnp.broadcast_to(row, (8, 128)))
        uvs.append(jnp.broadcast_to(aux_ref[source, pl.ds(slot % CAP, 1), :], (8, 128)))
        first = pl.multiple_of((slot % CAP) * 16, 16)
        vis = vis_ref[source, pl.ds(first, 16), :].astype(jnp.float32)
        res.append(vis[:8] * live)
        ims.append(vis[8:] * live)
        centre = base_col + ((code % COLS) * TILE).astype(jnp.float32)
        centres.append(jnp.full((8, 128), centre, jnp.float32))

    def stack(rows):
        return jnp.concatenate(rows, axis=0)

    ratio = stack([jnp.take_along_axis(r, spread, axis=1) for r in ratios])
    uv = stack(uvs)
    vu = stack([pltpu.roll(x, NV, 1) for x in uvs])
    low = stack([lane] * len(codes)) < NV
    fu = ratio * jnp.where(low, uv, vu)
    fv = ratio * jnp.where(low, vu, uv)
    x = fu * base_row
    y = fv * stack(centres)
    z = (x - jnp.round(x)) + (y - jnp.round(y))
    z = z - jnp.round(z)
    sh, ch = sincos_quarter(z * 0.5)
    sine = sh * ch * 2.0
    cosine = 1.0 - sh * sh * 2.0
    re, im = stack(res), stack(ims)
    amp_a = re * cosine - im * sine
    amp_b = re * sine + im * cosine

    def put(quantity, value):
        for g in range(len(codes)):
            keeps[g, quantity * 8 : quantity * 8 + 8, :] = value[g * 8 : g * 8 + 8]

    put(AMP_A, amp_a)
    put(AMP_B, amp_b)
    put(AMP_NA, -amp_a)
    put(AMP_NB, -amp_b)
    put(WEIGHT, (ratio - 1.0) * 10.0)
    theta_c, theta_s = harmonics(fu)
    phi_c, phi_s = harmonics(fv)
    for j in range(16):
        put(THETA_C + j, theta_c[j])
        put(THETA_S + j, theta_s[j])
        put(PHI_C + j, phi_c[j])
        put(PHI_S + j, phi_s[j])
    put(STEP, (phi_c[7] * phi_c[0] - phi_s[7] * phi_s[0]) * 2.0)
    put(THETA_STEP, (theta_c[7] * theta_c[0] - theta_s[7] * theta_s[0]) * 2.0)


def factors(keep, part):
    def eight(quantity):
        return keep[pl.ds(quantity * 8 + part, 8, stride=8), :]

    def one(quantity):
        return jnp.broadcast_to(keep[pl.ds(quantity * 8 + part, 1), :], (8, 128))

    def ladder(first, step, size):
        run = [eight(first), eight(first + 8)]
        for j in range(2, size):
            run.append(step * run[j - 1] - run[j - 2])
        return run

    weight = jnp.concatenate([one(WEIGHT)] * (HALF_P // 8), axis=0).astype(jnp.bfloat16)
    theta_step = one(THETA_STEP)
    theta_c = ladder(THETA_C, theta_step, HALF_P // 8)
    theta_s = ladder(THETA_S, theta_step, HALF_P // 8)
    kinds = ((AMP_A, theta_c), (AMP_NB, theta_s), (AMP_NA, theta_s), (AMP_NB, theta_c))
    left = []
    for amp, theta in kinds:
        gain = one(amp)
        plain = [gain * value for value in theta]
        plain = jnp.concatenate(plain, axis=0).astype(jnp.bfloat16)
        left += [plain, weight * plain]
    step = one(STEP)
    right = ladder(PHI_C, step, HALF_Q // 8) + ladder(PHI_S, step, HALF_Q // 8)
    return (
        jnp.concatenate(left, axis=0),
        jnp.concatenate(right, axis=0).astype(jnp.bfloat16),
    )


NT = (((1,), (1,)), ((), ()))


def product(keep):
    sums = [None, None]
    for part in range(0, 8, DEEP):
        made = [factors(keep, part + k) for k in range(DEEP)]
        left = jnp.concatenate([m[0] for m in made], axis=1)
        right = jnp.concatenate([m[1] for m in made], axis=1)
        for half in range(2):
            rows = slice(half * 2 * ROWS, half * 2 * ROWS + 2 * ROWS)
            cols = slice(half * HALF_Q, half * HALF_Q + HALF_Q)
            term = lax.dot_general(left[rows], right[cols], NT, preferred_element_type=jnp.float32)
            sums[half] = term if sums[half] is None else sums[half] + term
    return sums


def unfold_image(acc, lower_ref, upper_ref):
    lane = lax.broadcasted_iota(jnp.int32, (8, 128), 1)
    spread = jnp.where(lane < 64, 63 - lane, lane - 64)
    sign = jnp.where(lane < 64, -1.0, 1.0)
    turn = 7 - lax.broadcasted_iota(jnp.int32, (8, 128), 0)

    def unfold(even, odd):
        even = jnp.take_along_axis(even, spread, axis=1)
        return even + sign * jnp.take_along_axis(odd, spread, axis=1)

    def column(c, carry):
        lanes = pl.ds(pl.multiple_of(c * 128, 128), 128)
        for t in range(2):
            for j in range(HALF_P // 8):
                at = t * HALF_P + j * 8
                ee, oe, oo, eo = (acc[c, k * ROWS + at : k * ROWS + at + 8, :] for k in range(4))
                upper_ref[t, j * 8 : j * 8 + 8, lanes] = unfold(ee + oe, oo + eo)
                lower = unfold(ee - oe, eo - oo)
                to = HALF_P - 8 - j * 8
                lower_ref[t, to : to + 8, lanes] = jnp.take_along_axis(lower, turn, axis=0)
        return carry

    lax.fori_loop(0, COLS, column, 0)


def gridder(first, last, tile_ref, row_ref, place_ref, vis_ref, aux_ref, *rest):
    rest = list(rest)
    before = None if first else rest.pop(0)
    if last:
        own_ref, other_ref, acc = rest.pop(0), rest.pop(0), rest.pop(0)
    else:
        acc = rest.pop(0)
    keeps, work = rest
    acc[...] = jnp.zeros_like(acc) if first else before[...]
    my_row = row_ref[0]
    base_row = place_ref[0]
    base_col = place_ref[1]
    slots = tile_ref.shape[0]

    def visit(i, count):
        for k in range(8):
            slot = i * 8 + k
            tile = tile_ref[slot] - 1
            work[count] = slot * COLS + (tile & (COLS - 1))
            count = count + jnp.where((tile >> 4) == my_row, 1, 0)
        return count

    count = lax.fori_loop(0, slots // 8, visit, 0)
    for g in range(GROUP):
        work[count + g] = 0

    def step(i, carry):
        codes = [work[i * GROUP + g] for g in range(GROUP)]
        lives = [jnp.where(i * GROUP + g < count, 1.0 / 32.0, 0.0) for g in range(GROUP)]
        prepare(codes, lives, base_row, base_col, vis_ref, aux_ref, keeps)
        sums = [product(keeps.at[g]) for g in range(GROUP)]
        for g in range(GROUP):
            column = work[i * GROUP + g] % COLS
            for half in range(2):
                acc[column, half * 2 * ROWS : (half + 1) * 2 * ROWS, :HALF_Q] += sums[g][half]
        return carry

    lax.fori_loop(0, (count + GROUP - 1) // GROUP, step, 0)
    if last:

        @pl.when(row_ref[1] == 0)
        def _():
            unfold_image(acc, own_ref, other_ref)

        @pl.when(row_ref[1] != 0)
        def _():
            unfold_image(acc, other_ref, own_ref)


def grid_part(held, my_row, place, before, last):
    aux = held[:, CAP * 16 : PER, :].astype(jnp.float32)
    tiles = aux[:, 2, :CAP].astype(jnp.int32).reshape(-1)
    smem = pl.BlockSpec(memory_space=pltpu.SMEM)
    vmem = pl.BlockSpec(memory_space=pltpu.VMEM)
    first = before is None
    sums = jax.ShapeDtypeStruct((COLS, 4 * ROWS, TILE), jnp.float32)
    rows = jax.ShapeDtypeStruct((2, HALF_P, FCOLS), jnp.float32)
    operands = [tiles, my_row, place, held, aux] + ([] if first else [before])
    scratch = [
        pltpu.VMEM((GROUP, QUANTITIES * 8, 128), jnp.float32),
        pltpu.SMEM((tiles.shape[0] + GROUP + 4,), jnp.int32),
    ]
    expected = held.shape[0] * CAP // 4
    return pl.pallas_call(
        functools.partial(gridder, first, last),
        out_shape=(rows, rows) if last else sums,
        in_specs=[smem, smem, smem] + [vmem] * (len(operands) - 3),
        out_specs=(vmem, vmem) if last else vmem,
        scratch_shapes=([pltpu.VMEM(sums.shape, sums.dtype)] if last else []) + scratch,
        compiler_params=pltpu.CompilerParams(vmem_limit_bytes=32 * 1024 * 1024),
        cost_estimate=pl.CostEstimate(
            flops=expected * 200_000_000, bytes_accessed=held.size * 2, transcendentals=0
        ),
        name="gridder",
    )(*operands)


def packer(target_ref, tile_ref, ratio_ref, vis_ref, uv_ref, send_ref, rows, seen):
    facets = send_ref.shape[0]
    rows[...] = jnp.zeros_like(rows)
    for d in range(facets):
        seen[d] = 0
    value = ratio_ref[...]
    blank = jnp.zeros((1, 128 - CH), jnp.float32)
    for k in range(3):
        high = value.astype(jnp.bfloat16).astype(jnp.float32)
        value = value - high
        row = jnp.concatenate([high, blank], axis=1)
        for d in range(facets):
            rows[d, CAP * 17 + 1 + k : CAP * 17 + 2 + k, :] = row
    lane = lax.broadcasted_iota(jnp.int32, (1, 128), 1)
    for j in range(vis_ref.shape[1]):
        d = target_ref[0, j, 0]
        rank = jnp.minimum(seen[d], CAP - 1)
        seen[d] = rank + 1
        block = vis_ref[0, j].astype(jnp.float32)
        for c in range(8):
            for part in range(2):
                at = rank * 16 + part * 8 + c
                rows[d, pl.ds(at, 1), :] = block[part : part + 1, c * 128 : c * 128 + 128]
        uv = uv_ref[0, j].astype(jnp.float32)
        rows[d, pl.ds(CAP * 16 + rank, 1), :] = jnp.concatenate([uv[0:1], uv[1:2]], axis=1)
        tile = (tile_ref[0, j] + 1).astype(jnp.float32)
        rows[d, CAP * 17 : CAP * 17 + 1, :] += jnp.where(lane == rank, tile, 0.0)
    send_ref[...] = rows[...].astype(jnp.bfloat16)


def shards(visibilities, uv_coords, freq_ratio, target_facet, tile_index):
    facets = lax.axis_size("facet")
    bands = lax.axis_size("band")
    my_facet = lax.axis_index("facet")
    my_band = lax.axis_index("band")
    smem = pl.BlockSpec(memory_space=pltpu.SMEM)
    vmem = pl.BlockSpec(memory_space=pltpu.VMEM)
    send = pl.pallas_call(
        packer,
        out_shape=jax.ShapeDtypeStruct((facets, PER, 128), jnp.bfloat16),
        in_specs=[smem, smem, vmem, vmem, vmem],
        out_specs=vmem,
        scratch_shapes=[
            pltpu.VMEM((facets, PER, 128), jnp.float32),
            pltpu.SMEM((facets,), jnp.int32),
        ],
        name="packer",
    )(target_facet, tile_index, freq_ratio, visibilities, uv_coords)
    mine = lax.all_to_all(send, "facet", 0, 0, tiled=True)
    tile_row = my_band // (bands // (FROWS // TILE))
    my_row = jnp.stack([tile_row, my_band % 2]).astype(jnp.int32)
    place = jnp.stack(
        [
            FROWS * (my_facet % 4 - 2) + ROWS * (my_band // 2),
            FCOLS * (my_facet // 4 % 4 - 2),
        ]
    ).astype(jnp.float32) + jnp.array([(ROWS - 1) / 2, (TILE - 1) / 2], jnp.float32)

    def over_y(x):
        return lax.ppermute(x, "band", [(i, i ^ 8) for i in range(bands)])

    def over_core(x):
        return lax.ppermute(x, "band", [(i, i ^ 1) for i in range(bands)])

    def over_x(x, d):
        ring = [(i, i // 8 * 8 + (i % 8 // 2 + d) % 4 * 2 + i % 2) for i in range(bands)]
        return lax.ppermute(x, "band", ring)

    half = facets // 2
    from_y, from_up, from_down = over_y(mine), over_x(mine, 1), over_x(mine, 3)
    sums = grid_part(mine, my_row, place, None, False)
    from_up, from_down, sums = lax.optimization_barrier((from_up, from_down, sums))
    sides = jnp.concatenate([from_up, from_down], axis=0)
    opposite = [over_x(from_up[:half], 1), over_x(from_down[half:], 3)]
    across = over_y(sides)
    sums = grid_part(jnp.concatenate([from_y, sides], axis=0), my_row, place, sums, False)
    far = jnp.concatenate(opposite, axis=0)
    far, across, sums = lax.optimization_barrier((far, across, sums))
    farthest = over_y(far)
    sums = grid_part(jnp.concatenate([across, far], axis=0), my_row, place, sums, False)
    own, other = grid_part(farthest, my_row, place, sums, True)
    return (own + over_core(other))[None]


def solution(mesh):
    return jax.shard_map(
        shards,
        mesh=mesh,
        in_specs=(
            P("band", "facet", None, None),
            P("band", "facet", None, None),
            P("band", None),
            P("band", "facet", None),
            P("band", "facet"),
        ),
        out_specs=P("facet", None, "band", None),
        check_vma=False,
    )
```

```python
import functools

import jax
import jax.numpy as jnp
from jax import lax
from jax.experimental import pallas as pl
from jax.experimental.pallas import tpu as pltpu
from jax.sharding import PartitionSpec as P

TILE = 128
FCOLS = 2048
FROWS = 512
CAP = 2
CH = 16
NV = 64
ROWS = 64
HALF_P = ROWS // 2
HALF_Q = TILE // 2
COLS = FCOLS // TILE
PER = 40
GROUP = 4
RATIO_AT = 3
DEEP = 2

SIN = (
    6.28318530472, -41.3417013429, 81.6051561334, -76.7017195864, 41.9691302047, -14.1604742051
)
COS = (
    0.999999999208, -19.7392080649, 64.9392827706, -85.4506731816, 60.0909654249, -24.6453426591
)

PHI_C, PHI_S, THETA_C, THETA_S, AMP_A, AMP_B, AMP_NA, AMP_NB, WEIGHT, STEP, THETA_STEP = (
    0, 16, 32, 48, 64, 65, 66, 67, 68, 69, 70
)
QUANTITIES = 71


def horner(coefficients, x):
    total = jnp.full_like(x, coefficients[-1])
    for c in coefficients[-2::-1]:
        total = total * x + c
    return total


def sincos_quarter(x):
    square = x * x
    return x * horner(SIN, square), horner(COS, square)


def harmonics(cycles):
    s0, c0 = sincos_quarter(cycles * 0.5)
    double = c0 * c0 * 2.0 - 1.0
    sine = c0 * s0 * 2.0
    c1 = double * c0 - sine * s0
    s1 = sine * c0 + double * s0
    twice = double * double * 4.0 - 2.0
    cosines, sines = [c1, c0, c0, c1], [-s1, -s0, s0, s1]
    for j in range(4, 18):
        cosines.append(twice * cosines[j - 2] - cosines[j - 4])
        sines.append(twice * sines[j - 2] - sines[j - 4])
    return cosines[2:], sines[2:]


def prepare(codes, lives, base_row, base_col, vis_ref, aux_ref, keeps):
    lane = lax.broadcasted_iota(jnp.int32, (8, 128), 1)
    spread = lax.broadcasted_iota(jnp.int32, (8, 128), 0) * 2 + lane // NV
    ratios, uvs, res, ims, centres = [], [], [], [], []
    for code, live in zip(codes, lives):
        slot = code // COLS
        source = slot // CAP
        row = jnp.sum(aux_ref[source, RATIO_AT : RATIO_AT + 3, :], axis=0, keepdims=True)
        ratios.append(jnp.broadcast_to(row, (8, 128)))
        uvs.append(jnp.broadcast_to(aux_ref[source, pl.ds(slot % CAP, 1), :], (8, 128)))
        first = pl.multiple_of((slot % CAP) * 16, 16)
        vis = vis_ref[source, pl.ds(first, 16), :].astype(jnp.float32)
        res.append(vis[:8] * live)
        ims.append(vis[8:] * live)
        centre = base_col + ((code % COLS) * TILE).astype(jnp.float32)
        centres.append(jnp.full((8, 128), centre, jnp.float32))

    def stack(rows):
        return jnp.concatenate(rows, axis=0)

    ratio = stack([jnp.take_along_axis(r, spread, axis=1) for r in ratios])
    uv = stack(uvs)
    vu = stack([pltpu.roll(x, NV, 1) for x in uvs])
    low = stack([lane] * len(codes)) < NV
    fu = ratio * jnp.where(low, uv, vu)
    fv = ratio * jnp.where(low, vu, uv)
    x = fu * base_row
    y = fv * stack(centres)
    z = (x - jnp.round(x)) + (y - jnp.round(y))
    z = z - jnp.round(z)
    sh, ch = sincos_quarter(z * 0.5)
    sine = sh * ch * 2.0
    cosine = 1.0 - sh * sh * 2.0
    re, im = stack(res), stack(ims)
    amp_a = re * cosine - im * sine
    amp_b = re * sine + im * cosine

    def put(quantity, value):
        for g in range(len(codes)):
            keeps[g, quantity * 8 : quantity * 8 + 8, :] = value[g * 8 : g * 8 + 8]

    put(AMP_A, amp_a)
    put(AMP_B, amp_b)
    put(AMP_NA, -amp_a)
    put(AMP_NB, -amp_b)
    put(WEIGHT, (ratio - 1.0) * 10.0)
    theta_c, theta_s = harmonics(fu)
    phi_c, phi_s = harmonics(fv)
    for j in range(16):
        put(THETA_C + j, theta_c[j])
        put(THETA_S + j, theta_s[j])
        put(PHI_C + j, phi_c[j])
        put(PHI_S + j, phi_s[j])
    put(STEP, (phi_c[7] * phi_c[0] - phi_s[7] * phi_s[0]) * 2.0)
    put(THETA_STEP, (theta_c[7] * theta_c[0] - theta_s[7] * theta_s[0]) * 2.0)


def factors(keep, part):
    def eight(quantity):
        return keep[pl.ds(quantity * 8 + part, 8, stride=8), :]

    def one(quantity):
        return jnp.broadcast_to(keep[pl.ds(quantity * 8 + part, 1), :], (8, 128))

    def ladder(first, step, size):
        run = [eight(first), eight(first + 8)]
        for j in range(2, size):
            run.append(step * run[j - 1] - run[j - 2])
        return run

    weight = jnp.concatenate([one(WEIGHT)] * (HALF_P // 8), axis=0).astype(jnp.bfloat16)
    theta_step = one(THETA_STEP)
    theta_c = ladder(THETA_C, theta_step, HALF_P // 8)
    theta_s = ladder(THETA_S, theta_step, HALF_P // 8)
    kinds = ((AMP_A, theta_c), (AMP_NB, theta_s), (AMP_NA, theta_s), (AMP_NB, theta_c))
    left = []
    for amp, theta in kinds:
        gain = one(amp)
        plain = [gain * value for value in theta]
        plain = jnp.concatenate(plain, axis=0).astype(jnp.bfloat16)
        left += [plain, weight * plain]
    step = one(STEP)
    right = ladder(PHI_C, step, HALF_Q // 8) + ladder(PHI_S, step, HALF_Q // 8)
    return (
        jnp.concatenate(left, axis=0),
        jnp.concatenate(right, axis=0).astype(jnp.bfloat16),
    )


NT = (((1,), (1,)), ((), ()))


def product(keep):
    sums = [None, None]
    for part in range(0, 8, DEEP):
        made = [factors(keep, part + k) for k in range(DEEP)]
        left = jnp.concatenate([m[0] for m in made], axis=1)
        right = jnp.concatenate([m[1] for m in made], axis=1)
        for half in range(2):
            rows = slice(half * 2 * ROWS, half * 2 * ROWS + 2 * ROWS)
            cols = slice(half * HALF_Q, half * HALF_Q + HALF_Q)
            term = lax.dot_general(left[rows], right[cols], NT, preferred_element_type=jnp.float32)
            sums[half] = term if sums[half] is None else sums[half] + term
    return sums


def unfold_image(acc, lower_ref, upper_ref):
    lane = lax.broadcasted_iota(jnp.int32, (8, 128), 1)
    spread = jnp.where(lane < 64, 63 - lane, lane - 64)
    sign = jnp.where(lane < 64, -1.0, 1.0)
    turn = 7 - lax.broadcasted_iota(jnp.int32, (8, 128), 0)

    def unfold(even, odd):
        even = jnp.take_along_axis(even, spread, axis=1)
        return even + sign * jnp.take_along_axis(odd, spread, axis=1)

    def column(c, carry):
        lanes = pl.ds(pl.multiple_of(c * 128, 128), 128)
        for t in range(2):
            for j in range(HALF_P // 8):
                at = t * HALF_P + j * 8
                ee, oe, oo, eo = (acc[c, k * ROWS + at : k * ROWS + at + 8, :] for k in range(4))
                upper_ref[t, j * 8 : j * 8 + 8, lanes] = unfold(ee + oe, oo + eo)
                lower = unfold(ee - oe, eo - oo)
                to = HALF_P - 8 - j * 8
                lower_ref[t, to : to + 8, lanes] = jnp.take_along_axis(lower, turn, axis=0)
        return carry

    lax.fori_loop(0, COLS, column, 0)


def gridder(first, last, tile_ref, row_ref, place_ref, vis_ref, aux_ref, *rest):
    rest = list(rest)
    before = None if first else rest.pop(0)
    if last:
        own_ref, other_ref, acc = rest.pop(0), rest.pop(0), rest.pop(0)
    else:
        acc = rest.pop(0)
    keeps, work = rest
    acc[...] = jnp.zeros_like(acc) if first else before[...]
    my_row = row_ref[0]
    base_row = place_ref[0]
    base_col = place_ref[1]
    slots = tile_ref.shape[0]

    def visit(i, count):
        for k in range(8):
            slot = i * 8 + k
            tile = tile_ref[slot] - 1
            work[count] = slot * COLS + (tile & (COLS - 1))
            count = count + jnp.where((tile >> 4) == my_row, 1, 0)
        return count

    count = lax.fori_loop(0, slots // 8, visit, 0)
    for g in range(GROUP):
        work[count + g] = 0

    def step(i, carry):
        codes = [work[i * GROUP + g] for g in range(GROUP)]
        lives = [jnp.where(i * GROUP + g < count, 1.0 / 32.0, 0.0) for g in range(GROUP)]
        prepare(codes, lives, base_row, base_col, vis_ref, aux_ref, keeps)
        sums = [product(keeps.at[g]) for g in range(GROUP)]
        for g in range(GROUP):
            column = work[i * GROUP + g] % COLS
            for half in range(2):
                acc[column, half * 2 * ROWS : (half + 1) * 2 * ROWS, :HALF_Q] += sums[g][half]
        return carry

    lax.fori_loop(0, (count + GROUP - 1) // GROUP, step, 0)
    if last:

        @pl.when(row_ref[1] == 0)
        def _():
            unfold_image(acc, own_ref, other_ref)

        @pl.when(row_ref[1] != 0)
        def _():
            unfold_image(acc, other_ref, own_ref)


def grid_part(held, my_row, place, before, last):
    aux = held[:, CAP * 16 : PER, :].astype(jnp.float32)
    tiles = aux[:, 2, :CAP].astype(jnp.int32).reshape(-1)
    smem = pl.BlockSpec(memory_space=pltpu.SMEM)
    vmem = pl.BlockSpec(memory_space=pltpu.VMEM)
    first = before is None
    sums = jax.ShapeDtypeStruct((COLS, 4 * ROWS, TILE), jnp.float32)
    rows = jax.ShapeDtypeStruct((2, HALF_P, FCOLS), jnp.float32)
    operands = [tiles, my_row, place, held, aux] + ([] if first else [before])
    scratch = [
        pltpu.VMEM((GROUP, QUANTITIES * 8, 128), jnp.float32),
        pltpu.SMEM((tiles.shape[0] + GROUP + 4,), jnp.int32),
    ]
    expected = held.shape[0] * CAP // 4
    return pl.pallas_call(
        functools.partial(gridder, first, last),
        out_shape=(rows, rows) if last else sums,
        in_specs=[smem, smem, smem] + [vmem] * (len(operands) - 3),
        out_specs=(vmem, vmem) if last else vmem,
        scratch_shapes=([pltpu.VMEM(sums.shape, sums.dtype)] if last else []) + scratch,
        compiler_params=pltpu.CompilerParams(vmem_limit_bytes=14 * 1024 * 1024),
        cost_estimate=pl.CostEstimate(
            flops=expected * 200_000_000, bytes_accessed=held.size * 2, transcendentals=0
        ),
        name="gridder",
    )(*operands)


def packer(target_ref, tile_ref, ratio_ref, vis_ref, uv_ref, send_ref, rows, seen):
    facets = send_ref.shape[0]
    rows[...] = jnp.zeros_like(rows)
    for d in range(facets):
        seen[d] = 0
    value = ratio_ref[...]
    blank = jnp.zeros((1, 128 - CH), jnp.float32)
    for k in range(3):
        high = value.astype(jnp.bfloat16).astype(jnp.float32)
        value = value - high
        row = jnp.concatenate([high, blank], axis=1)
        for d in range(facets):
            rows[d, CAP * 17 + 1 + k : CAP * 17 + 2 + k, :] = row
    lane = lax.broadcasted_iota(jnp.int32, (1, 128), 1)
    for j in range(vis_ref.shape[1]):
        d = target_ref[0, j]
        rank = jnp.minimum(seen[d], CAP - 1)
        seen[d] = rank + 1
        block = vis_ref[0, j].astype(jnp.float32)
        for c in range(8):
            for part in range(2):
                at = rank * 16 + part * 8 + c
                rows[d, pl.ds(at, 1), :] = block[part : part + 1, c * 128 : c * 128 + 128]
        uv = uv_ref[0, j].astype(jnp.float32)
        rows[d, pl.ds(CAP * 16 + rank, 1), :] = jnp.concatenate([uv[0:1], uv[1:2]], axis=1)
        tile = (tile_ref[0, j] + 1).astype(jnp.float32)
        rows[d, CAP * 17 : CAP * 17 + 1, :] += jnp.where(lane == rank, tile, 0.0)
    send_ref[...] = rows[...].astype(jnp.bfloat16)


def shards(visibilities, uv_coords, freq_ratio, target_facet, tile_index):
    facets = lax.axis_size("facet")
    bands = lax.axis_size("band")
    my_facet = lax.axis_index("facet")
    my_band = lax.axis_index("band")
    smem = pl.BlockSpec(memory_space=pltpu.SMEM)
    vmem = pl.BlockSpec(memory_space=pltpu.VMEM)
    send = pl.pallas_call(
        packer,
        out_shape=jax.ShapeDtypeStruct((facets, PER, 128), jnp.bfloat16),
        in_specs=[smem, smem, vmem, vmem, vmem],
        out_specs=vmem,
        scratch_shapes=[
            pltpu.VMEM((facets, PER, 128), jnp.float32),
            pltpu.SMEM((facets,), jnp.int32),
        ],
        name="packer",
    )(target_facet[:, :, 0], tile_index, freq_ratio, visibilities, uv_coords)
    mine = lax.all_to_all(send, "facet", 0, 0, tiled=True)
    tile_row = my_band // (bands // (FROWS // TILE))
    my_row = jnp.stack([tile_row, my_band % 2]).astype(jnp.int32)
    place = jnp.stack(
        [
            FROWS * (my_facet % 4 - 2) + ROWS * (my_band // 2),
            FCOLS * (my_facet // 4 % 4 - 2),
        ]
    ).astype(jnp.float32) + jnp.array([(ROWS - 1) / 2, (TILE - 1) / 2], jnp.float32)

    def over_y(x):
        return lax.ppermute(x, "band", [(i, i ^ 8) for i in range(bands)])

    def over_core(x):
        return lax.ppermute(x, "band", [(i, i ^ 1) for i in range(bands)])

    def over_x(x, d):
        ring = [(i, i // 8 * 8 + (i % 8 // 2 + d) % 4 * 2 + i % 2) for i in range(bands)]
        return lax.ppermute(x, "band", ring)

    half = facets // 2
    from_y, from_up, from_down = over_y(mine), over_x(mine, 1), over_x(mine, 3)
    sums = grid_part(mine, my_row, place, None, False)
    from_up, from_down, sums = lax.optimization_barrier((from_up, from_down, sums))
    sides = jnp.concatenate([from_up, from_down], axis=0)
    opposite = [over_x(from_up[:half], 1), over_x(from_down[half:], 3)]
    across = over_y(sides)
    sums = grid_part(jnp.concatenate([from_y, sides], axis=0), my_row, place, sums, False)
    far = jnp.concatenate(opposite, axis=0)
    far, across, sums = lax.optimization_barrier((far, across, sums))
    farthest = over_y(far)
    sums = grid_part(jnp.concatenate([across, far], axis=0), my_row, place, sums, False)
    own, other = grid_part(farthest, my_row, place, sums, True)
    return (own + over_core(other))[None]


def solution(mesh):
    return jax.shard_map(
        shards,
        mesh=mesh,
        in_specs=(
            P("band", "facet", None, None),
            P("band", "facet", None, None),
            P("band", None),
            P("band", "facet", None),
            P("band", "facet"),
        ),
        out_specs=P("facet", None, "band", None),
        check_vma=False,
    )
```

```python
import functools

import jax
import jax.numpy as jnp
from jax import lax
from jax.experimental import pallas as pl
from jax.experimental.pallas import tpu as pltpu
from jax.sharding import PartitionSpec as P

TILE = 128
FCOLS = 2048
FROWS = 512
CAP = 2
CH = 16
NV = 64
ROWS = 64
HALF_P = ROWS // 2
HALF_Q = TILE // 2
COLS = FCOLS // TILE
PER = 40
GROUP = 4
RATIO_AT = 3
DEEP = 4

SIN = (
    6.28318530472, -41.3417013429, 81.6051561334, -76.7017195864, 41.9691302047, -14.1604742051
)
COS = (
    0.999999999208, -19.7392080649, 64.9392827706, -85.4506731816, 60.0909654249, -24.6453426591
)

PHI_C, PHI_S, THETA_C, THETA_S, AMP_A, AMP_B, AMP_NA, AMP_NB, WEIGHT, STEP, THETA_STEP = (
    0, 16, 32, 48, 64, 65, 66, 67, 68, 69, 70
)
QUANTITIES = 71


def horner(coefficients, x):
    total = jnp.full_like(x, coefficients[-1])
    for c in coefficients[-2::-1]:
        total = total * x + c
    return total


def sincos_quarter(x):
    square = x * x
    return x * horner(SIN, square), horner(COS, square)


def harmonics(cycles):
    s0, c0 = sincos_quarter(cycles * 0.5)
    double = c0 * c0 * 2.0 - 1.0
    sine = c0 * s0 * 2.0
    c1 = double * c0 - sine * s0
    s1 = sine * c0 + double * s0
    twice = double * double * 4.0 - 2.0
    cosines, sines = [c1, c0, c0, c1], [-s1, -s0, s0, s1]
    for j in range(4, 18):
        cosines.append(twice * cosines[j - 2] - cosines[j - 4])
        sines.append(twice * sines[j - 2] - sines[j - 4])
    return cosines[2:], sines[2:]


def prepare(codes, lives, base_row, base_col, vis_ref, aux_ref, keeps):
    lane = lax.broadcasted_iota(jnp.int32, (8, 128), 1)
    spread = lax.broadcasted_iota(jnp.int32, (8, 128), 0) * 2 + lane // NV
    ratios, uvs, res, ims, centres = [], [], [], [], []
    for code, live in zip(codes, lives):
        slot = code // COLS
        source = slot // CAP
        row = jnp.sum(aux_ref[source, RATIO_AT : RATIO_AT + 3, :], axis=0, keepdims=True)
        ratios.append(jnp.broadcast_to(row, (8, 128)))
        uvs.append(jnp.broadcast_to(aux_ref[source, pl.ds(slot % CAP, 1), :], (8, 128)))
        first = pl.multiple_of((slot % CAP) * 16, 16)
        vis = vis_ref[source, pl.ds(first, 16), :].astype(jnp.float32)
        res.append(vis[:8] * live)
        ims.append(vis[8:] * live)
        centre = base_col + ((code % COLS) * TILE).astype(jnp.float32)
        centres.append(jnp.full((8, 128), centre, jnp.float32))

    def stack(rows):
        return jnp.concatenate(rows, axis=0)

    ratio = stack([jnp.take_along_axis(r, spread, axis=1) for r in ratios])
    uv = stack(uvs)
    vu = stack([pltpu.roll(x, NV, 1) for x in uvs])
    low = stack([lane] * len(codes)) < NV
    fu = ratio * jnp.where(low, uv, vu)
    fv = ratio * jnp.where(low, vu, uv)
    x = fu * base_row
    y = fv * stack(centres)
    z = (x - jnp.round(x)) + (y - jnp.round(y))
    z = z - jnp.round(z)
    sh, ch = sincos_quarter(z * 0.5)
    sine = sh * ch * 2.0
    cosine = 1.0 - sh * sh * 2.0
    re, im = stack(res), stack(ims)
    amp_a = re * cosine - im * sine
    amp_b = re * sine + im * cosine

    def put(quantity, value):
        for g in range(len(codes)):
            keeps[g, quantity * 8 : quantity * 8 + 8, :] = value[g * 8 : g * 8 + 8]

    put(AMP_A, amp_a)
    put(AMP_B, amp_b)
    put(AMP_NA, -amp_a)
    put(AMP_NB, -amp_b)
    put(WEIGHT, (ratio - 1.0) * 10.0)
    theta_c, theta_s = harmonics(fu)
    phi_c, phi_s = harmonics(fv)
    for j in range(16):
        put(THETA_C + j, theta_c[j])
        put(THETA_S + j, theta_s[j])
        put(PHI_C + j, phi_c[j])
        put(PHI_S + j, phi_s[j])
    put(STEP, (phi_c[7] * phi_c[0] - phi_s[7] * phi_s[0]) * 2.0)
    put(THETA_STEP, (theta_c[7] * theta_c[0] - theta_s[7] * theta_s[0]) * 2.0)


def factors(keep, part):
    def eight(quantity):
        return keep[pl.ds(quantity * 8 + part, 8, stride=8), :]

    def one(quantity):
        return jnp.broadcast_to(keep[pl.ds(quantity * 8 + part, 1), :], (8, 128))

    def ladder(first, step, size):
        run = [eight(first), eight(first + 8)]
        for j in range(2, size):
            run.append(step * run[j - 1] - run[j - 2])
        return run

    weight = jnp.concatenate([one(WEIGHT)] * (HALF_P // 8), axis=0).astype(jnp.bfloat16)
    theta_step = one(THETA_STEP)
    theta_c = ladder(THETA_C, theta_step, HALF_P // 8)
    theta_s = ladder(THETA_S, theta_step, HALF_P // 8)
    kinds = ((AMP_A, theta_c), (AMP_NB, theta_s), (AMP_NA, theta_s), (AMP_NB, theta_c))
    left = []
    for amp, theta in kinds:
        gain = one(amp)
        plain = [gain * value for value in theta]
        plain = jnp.concatenate(plain, axis=0).astype(jnp.bfloat16)
        left += [plain, weight * plain]
    step = one(STEP)
    right = ladder(PHI_C, step, HALF_Q // 8) + ladder(PHI_S, step, HALF_Q // 8)
    return (
        jnp.concatenate(left, axis=0),
        jnp.concatenate(right, axis=0).astype(jnp.bfloat16),
    )


NT = (((1,), (1,)), ((), ()))


def product(keep):
    sums = [None, None]
    for part in range(0, 8, DEEP):
        made = [factors(keep, part + k) for k in range(DEEP)]
        left = jnp.concatenate([m[0] for m in made], axis=1)
        right = jnp.concatenate([m[1] for m in made], axis=1)
        for half in range(2):
            rows = slice(half * 2 * ROWS, half * 2 * ROWS + 2 * ROWS)
            cols = slice(half * HALF_Q, half * HALF_Q + HALF_Q)
            term = lax.dot_general(left[rows], right[cols], NT, preferred_element_type=jnp.float32)
            sums[half] = term if sums[half] is None else sums[half] + term
    return sums


def unfold_image(acc, lower_ref, upper_ref):
    lane = lax.broadcasted_iota(jnp.int32, (8, 128), 1)
    spread = jnp.where(lane < 64, 63 - lane, lane - 64)
    sign = jnp.where(lane < 64, -1.0, 1.0)
    turn = 7 - lax.broadcasted_iota(jnp.int32, (8, 128), 0)

    def unfold(even, odd):
        even = jnp.take_along_axis(even, spread, axis=1)
        return even + sign * jnp.take_along_axis(odd, spread, axis=1)

    def column(c, carry):
        lanes = pl.ds(pl.multiple_of(c * 128, 128), 128)
        for t in range(2):
            for j in range(HALF_P // 8):
                at = t * HALF_P + j * 8
                ee, oe, oo, eo = (acc[c, k * ROWS + at : k * ROWS + at + 8, :] for k in range(4))
                upper_ref[t, j * 8 : j * 8 + 8, lanes] = unfold(ee + oe, oo + eo)
                lower = unfold(ee - oe, eo - oo)
                to = HALF_P - 8 - j * 8
                lower_ref[t, to : to + 8, lanes] = jnp.take_along_axis(lower, turn, axis=0)
        return carry

    lax.fori_loop(0, COLS, column, 0)


def gridder(first, last, tile_ref, row_ref, place_ref, vis_ref, aux_ref, *rest):
    rest = list(rest)
    before = None if first else rest.pop(0)
    if last:
        own_ref, other_ref, acc = rest.pop(0), rest.pop(0), rest.pop(0)
    else:
        acc = rest.pop(0)
    keeps, work = rest
    acc[...] = jnp.zeros_like(acc) if first else before[...]
    my_row = row_ref[0]
    base_row = place_ref[0]
    base_col = place_ref[1]
    slots = tile_ref.shape[0]

    def visit(i, count):
        for k in range(8):
            slot = i * 8 + k
            tile = tile_ref[slot] - 1
            work[count] = slot * COLS + (tile & (COLS - 1))
            count = count + jnp.where((tile >> 4) == my_row, 1, 0)
        return count

    count = lax.fori_loop(0, slots // 8, visit, 0)
    for g in range(GROUP):
        work[count + g] = 0

    def step(i, carry):
        codes = [work[i * GROUP + g] for g in range(GROUP)]
        lives = [jnp.where(i * GROUP + g < count, 1.0 / 32.0, 0.0) for g in range(GROUP)]
        prepare(codes, lives, base_row, base_col, vis_ref, aux_ref, keeps)
        sums = [product(keeps.at[g]) for g in range(GROUP)]
        for g in range(GROUP):
            column = work[i * GROUP + g] % COLS
            for half in range(2):
                acc[column, half * 2 * ROWS : (half + 1) * 2 * ROWS, :HALF_Q] += sums[g][half]
        return carry

    lax.fori_loop(0, (count + GROUP - 1) // GROUP, step, 0)
    if last:

        @pl.when(row_ref[1] == 0)
        def _():
            unfold_image(acc, own_ref, other_ref)

        @pl.when(row_ref[1] != 0)
        def _():
            unfold_image(acc, other_ref, own_ref)


def grid_part(held, my_row, place, before, last):
    aux = held[:, CAP * 16 : PER, :].astype(jnp.float32)
    tiles = aux[:, 2, :CAP].astype(jnp.int32).reshape(-1)
    smem = pl.BlockSpec(memory_space=pltpu.SMEM)
    vmem = pl.BlockSpec(memory_space=pltpu.VMEM)
    first = before is None
    sums = jax.ShapeDtypeStruct((COLS, 4 * ROWS, TILE), jnp.float32)
    rows = jax.ShapeDtypeStruct((2, HALF_P, FCOLS), jnp.float32)
    operands = [tiles, my_row, place, held, aux] + ([] if first else [before])
    scratch = [
        pltpu.VMEM((GROUP, QUANTITIES * 8, 128), jnp.float32),
        pltpu.SMEM((tiles.shape[0] + GROUP + 4,), jnp.int32),
    ]
    expected = held.shape[0] * CAP // 4
    return pl.pallas_call(
        functools.partial(gridder, first, last),
        out_shape=(rows, rows) if last else sums,
        in_specs=[smem, smem, smem] + [vmem] * (len(operands) - 3),
        out_specs=(vmem, vmem) if last else vmem,
        scratch_shapes=([pltpu.VMEM(sums.shape, sums.dtype)] if last else []) + scratch,
        compiler_params=pltpu.CompilerParams(vmem_limit_bytes=14 * 1024 * 1024),
        cost_estimate=pl.CostEstimate(
            flops=expected * 200_000_000, bytes_accessed=held.size * 2, transcendentals=0
        ),
        name="gridder",
    )(*operands)


def packer(target_ref, tile_ref, ratio_ref, vis_ref, uv_ref, send_ref, rows, seen):
    facets = send_ref.shape[0]
    rows[...] = jnp.zeros_like(rows)
    for d in range(facets):
        seen[d] = 0
    value = ratio_ref[...]
    blank = jnp.zeros((1, 128 - CH), jnp.float32)
    for k in range(3):
        high = value.astype(jnp.bfloat16).astype(jnp.float32)
        value = value - high
        row = jnp.concatenate([high, blank], axis=1)
        for d in range(facets):
            rows[d, CAP * 17 + 1 + k : CAP * 17 + 2 + k, :] = row
    lane = lax.broadcasted_iota(jnp.int32, (1, 128), 1)
    for j in range(vis_ref.shape[1]):
        d = target_ref[0, j]
        rank = jnp.minimum(seen[d], CAP - 1)
        seen[d] = rank + 1
        block = vis_ref[0, j].astype(jnp.float32)
        for c in range(8):
            for part in range(2):
                at = rank * 16 + part * 8 + c
                rows[d, pl.ds(at, 1), :] = block[part : part + 1, c * 128 : c * 128 + 128]
        uv = uv_ref[0, j].astype(jnp.float32)
        rows[d, pl.ds(CAP * 16 + rank, 1), :] = jnp.concatenate([uv[0:1], uv[1:2]], axis=1)
        tile = (tile_ref[0, j] + 1).astype(jnp.float32)
        rows[d, CAP * 17 : CAP * 17 + 1, :] += jnp.where(lane == rank, tile, 0.0)
    send_ref[...] = rows[...].astype(jnp.bfloat16)


def shards(visibilities, uv_coords, freq_ratio, target_facet, tile_index):
    facets = lax.axis_size("facet")
    bands = lax.axis_size("band")
    my_facet = lax.axis_index("facet")
    my_band = lax.axis_index("band")
    smem = pl.BlockSpec(memory_space=pltpu.SMEM)
    vmem = pl.BlockSpec(memory_space=pltpu.VMEM)
    send = pl.pallas_call(
        packer,
        out_shape=jax.ShapeDtypeStruct((facets, PER, 128), jnp.bfloat16),
        in_specs=[smem, smem, vmem, vmem, vmem],
        out_specs=vmem,
        scratch_shapes=[
            pltpu.VMEM((facets, PER, 128), jnp.float32),
            pltpu.SMEM((facets,), jnp.int32),
        ],
        name="packer",
    )(target_facet[:, :, 0], tile_index, freq_ratio, visibilities, uv_coords)
    mine = lax.all_to_all(send, "facet", 0, 0, tiled=True)
    tile_row = my_band // (bands // (FROWS // TILE))
    my_row = jnp.stack([tile_row, my_band % 2]).astype(jnp.int32)
    place = jnp.stack(
        [
            FROWS * (my_facet % 4 - 2) + ROWS * (my_band // 2),
            FCOLS * (my_facet // 4 % 4 - 2),
        ]
    ).astype(jnp.float32) + jnp.array([(ROWS - 1) / 2, (TILE - 1) / 2], jnp.float32)

    def over_y(x):
        return lax.ppermute(x, "band", [(i, i ^ 8) for i in range(bands)])

    def over_core(x):
        return lax.ppermute(x, "band", [(i, i ^ 1) for i in range(bands)])

    def over_x(x, d):
        ring = [(i, i // 8 * 8 + (i % 8 // 2 + d) % 4 * 2 + i % 2) for i in range(bands)]
        return lax.ppermute(x, "band", ring)

    half = facets // 2
    from_y, from_up, from_down = over_y(mine), over_x(mine, 1), over_x(mine, 3)
    sums = grid_part(mine, my_row, place, None, False)
    from_up, from_down, sums = lax.optimization_barrier((from_up, from_down, sums))
    sides = jnp.concatenate([from_up, from_down], axis=0)
    opposite = [over_x(from_up[:half], 1), over_x(from_down[half:], 3)]
    across = over_y(sides)
    sums = grid_part(jnp.concatenate([from_y, sides], axis=0), my_row, place, sums, False)
    far = jnp.concatenate(opposite, axis=0)
    far, across, sums = lax.optimization_barrier((far, across, sums))
    farthest = over_y(far)
    sums = grid_part(jnp.concatenate([across, far], axis=0), my_row, place, sums, False)
    own, other = grid_part(farthest, my_row, place, sums, True)
    return (own + over_core(other))[None]


def solution(mesh):
    return jax.shard_map(
        shards,
        mesh=mesh,
        in_specs=(
            P("band", "facet", None, None),
            P("band", "facet", None, None),
            P("band", None),
            P("band", "facet", None),
            P("band", "facet"),
        ),
        out_specs=P("facet", None, "band", None),
        check_vma=False,
    )
```
